512 devices in a mesh: prow: 4 (over x_lo, core), pcol: 128 (over z, y, x_hi).
Axes of the slice: x: 4 (x_hi: 2, x_lo: 2; x = x_hi * 2 + x_lo), y: 8, z: 8, core: 2. Of those that a mesh axis runs over, the one named last changes fastest.
Arguments:
- matrix: bfloat16 [12288, 12288], P('prow', 'pcol'), may hold values from -8 to 8
- vectors_one: bfloat16 [12288, 256], P('prow'), may hold values from -1 to 1, as said below
- factor_one: float32 [256, 256], replicated, may hold values from -1 to 2, as said below
- vectors_two: bfloat16 [12288, 256], P('prow'), may hold values from -1 to 1, as said below
- factor_two: float32 [256, 256], replicated, may hold values from -1 to 2, as said below
Outputs:
- reduced: bfloat16 [12288, 12288], P('prow', 'pcol')
The draws below stay inside these ranges and needn't reach their ends.
Inputs may be any that keep to these rules, and one draw needn't show every extreme that they name: `vectors_one`: column j is zero in rows above 256 + j, one in row 256 + j. `vectors_two`: column j is zero in rows above 512 + j, one in row 512 + j. `factor_one`: upper triangular. `factor_two`: upper triangular.
All inputs are finite; a program needn't handle non-finite values.
Results may differ from the reference program's by a relative error of at most 0.0055.
Values may be sent and summed in bfloat16 or wider, within the bound.
A program may use at most 64 MiB of HBM per device.

```python
import jax
import jax.numpy as jnp
from jax import lax

B = 256
N = 12288


def reflectors(key, leading):
    row_ids = lax.broadcasted_iota(jnp.int32, (N, B), 0)
    col_ids = lax.broadcasted_iota(jnp.int32, (N, B), 1)
    noise = jnp.clip(jax.random.normal(key, (N, B), jnp.float32), -5.0, 5.0) * N ** (-0.5)
    head = leading + col_ids
    return jnp.where(row_ids < head, 0.0, jnp.where(row_ids == head, 1.0, noise))


def triangle(key):
    first, second = jax.random.split(key)
    diag_vals = jax.random.uniform(first, (B,), jnp.float32, 1.0, 2.0)
    upper = jnp.clip(jax.random.normal(second, (B, B), jnp.float32), -5.0, 5.0) * (0.5 * B ** (-0.5))
    row_ids = lax.broadcasted_iota(jnp.int32, (B, B), 0)
    col_ids = lax.broadcasted_iota(jnp.int32, (B, B), 1)
    upper = jnp.where(col_ids > row_ids, upper, 0.0)
    return upper + jnp.diag(diag_vals)


def draw_matrix(key, part):
    key = jax.random.fold_in(key, 5)
    base = jnp.clip(jax.random.normal(key, (N, N), jnp.float32), -5.0, 5.0)
    return ((base + base.T) * 0.7071).astype(jnp.bfloat16)


def draw_vectors_one(key, part):
    key = jax.random.fold_in(key, 1)
    return reflectors(key, B).astype(jnp.bfloat16)


def draw_vectors_two(key, part):
    key = jax.random.fold_in(key, 2)
    return reflectors(key, 2 * B).astype(jnp.bfloat16)


def draw_factor_one(key, part):
    key = jax.random.fold_in(key, 3)
    return triangle(key)


def draw_factor_two(key, part):
    key = jax.random.fold_in(key, 4)
    return triangle(key)


def setup_inputs(seed: int = 0) -> dict:
    key_list = jax.random.split(jax.random.key(seed), 6)
    matrix = draw_matrix(jax.random.fold_in(key_list[5], 71), 0)
    vectors_one = draw_vectors_one(jax.random.fold_in(key_list[5], 71), 0)
    factor_one = draw_factor_one(jax.random.fold_in(key_list[5], 71), 0)
    vectors_two = draw_vectors_two(jax.random.fold_in(key_list[5], 71), 0)
    factor_two = draw_factor_two(jax.random.fold_in(key_list[5], 71), 0)
    return {"matrix": matrix, "vectors_one": vectors_one, "factor_one": factor_one, "vectors_two": vectors_two, "factor_two": factor_two}


def panel_update(current, vectors, factor):
    high = lax.Precision.HIGHEST
    sums = jnp.dot(current, vectors, preferred_element_type=jnp.float32)
    product = jnp.dot(sums, factor, precision=high)
    wide_vectors = vectors.astype(jnp.float32)
    inner = jnp.dot(wide_vectors.T, product, precision=high)
    wide = product - 0.5 * jnp.dot(wide_vectors, jnp.dot(factor.T, inner, precision=high), precision=high)
    wide = wide.astype(jnp.bfloat16)
    update = jnp.dot(vectors, wide.T, preferred_element_type=jnp.float32) + jnp.dot(wide, vectors.T, preferred_element_type=jnp.float32)
    return (current.astype(jnp.float32) - update).astype(jnp.bfloat16)


def reference(matrix, vectors_one, factor_one, vectors_two, factor_two):
    current = panel_update(matrix, vectors_one, factor_one)
    return panel_update(current, vectors_two, factor_two)
```

```python
import functools

import jax
import jax.numpy as jnp
from jax import lax
from jax.experimental import pallas as pl
from jax.experimental.pallas import tpu as pltpu
from jax.sharding import PartitionSpec as P

MESH = pl.DeviceIdType.MESH
HIGH = lax.Precision.HIGHEST
PARTS = (8, 8, 2)
ROWS = 4
F32 = jnp.float32
BF16 = jnp.bfloat16


def dot(lhs, rhs, left=1, right=0, precision=None):
    return lax.dot_general(
        lhs, rhs, (((left,), (right,)), ((), ())), precision=precision, preferred_element_type=F32
    )


def kernel(
    parts,
    a_hbm, v1_hbm, v2_hbm, f1_hbm, f2_hbm,
    out,
    a, v, f, term, rs_buf, s_buf, unit, s, cols, cross, cross_buf, cross_far, at, base, hacc, h_buf, h_send, h_far,
    load, rs_tx, rs_rx, vc_tx, vc_rx, sg_tx, sg_rx, sc_tx, sc_rx, c_tx, c_rx, h_tx, h_rx,
    y_tx, y_rx, z_tx, z_rx, ring_tx, ring_rx,
):
    nz, ny, nh = parts
    depth = nz // ROWS
    half_rows, panel = unit.shape
    width = 2 * half_rows
    p = lax.axis_index("prow")
    q = lax.axis_index("pcol")
    z, y, h = q // (ny * nh), (q // nh) % ny, q % nh
    lo, core = p // 2, p % 2
    mates = (2 * lo + 1 - core, 2 * (1 - lo) + core, 3 - p)

    def at_device(row, zi, yi, hi):
        return {"prow": row, "pcol": (zi * ny + yi) * nh + hi}

    def peer(k):
        return {"prow": mates[k], "pcol": q}

    def remote(src, dst, tx, rx, device):
        return pltpu.make_async_remote_copy(
            src_ref=src, dst_ref=dst, send_sem=tx, recv_sem=rx, device_id=device, device_id_type=MESH
        )

    owner, slab = z // depth, z % depth
    my_slab, my_piece = z // 4, z % 4
    to_z = (slab * 2 + h) * 2 + lo
    stays = (owner == p) & (to_z == z)
    from_z, from_h, from_lo = p * depth + my_slab, my_piece // 2, my_piece % 2

    loads = [
        pltpu.make_async_copy(a_hbm, a, load.at[0]),
        pltpu.make_async_copy(v1_hbm, v.at[0], load.at[1]),
        pltpu.make_async_copy(v2_hbm, v.at[1], load.at[2]),
        pltpu.make_async_copy(f1_hbm, f.at[0], load.at[3]),
        pltpu.make_async_copy(f2_hbm, f.at[1], load.at[4]),
    ]
    for copy in loads:
        copy.start()

    barrier = pltpu.get_barrier_semaphore()

    def greet(device):
        pl.semaphore_signal(barrier, inc=1, device_id=device, device_id_type=MESH)

    for k in range(3):
        greet(peer(k))
    for k in range(1, ny):
        greet(at_device(p, z, (y + k) % ny, h))
    for k in range(1, nz):
        greet(at_device(p, (z + k) % nz, y, h))
    for panel_id in range(2):
        from_p = from_lo * 2 + panel_id

        @pl.when(jnp.logical_not((from_p == p) & (from_z == z) & (from_h == h)))
        def _():
            greet(at_device(from_p, from_z, y, from_h))

    for copy in loads[:3]:
        copy.wait()
    rows = v.shape[1] * v.shape[2] * v.shape[3] * v.shape[4]
    for panel_id in range(2):
        part = dot(a[...], v[panel_id].reshape(rows, panel), 0, 0)
        term[panel_id] = part.reshape(2, half_rows, panel)

    expected = 3 + (ny - 1) + (nz - 1) + 2 - jnp.where(stays, 1, 0)
    pl.semaphore_wait(barrier, expected)

    scattered = []
    for k in (2, 1, 0):
        mate = mates[k]
        copy = remote(term.at[mate % 2, mate // 2], rs_buf.at[k], rs_tx.at[k], rs_rx.at[k], peer(k))
        copy.start()
        scattered.append(copy)

    mine = v.at[:, slab, y, pl.ds(2 * h, 2)]
    col_copies = [remote(mine, cols, vc_tx.at[k], vc_rx, peer(k)) for k in range(3)]
    col_local = pltpu.make_async_copy(mine, cols, vc_rx)

    @pl.when(owner == p)
    def _():
        for copy in col_copies:
            copy.start()
        col_local.start()

    cross[...] = dot(v[0].reshape(rows, panel), v[1].reshape(rows, panel), 0, 0)
    cross_near = remote(cross, cross_buf, c_tx.at[0], c_rx.at[0], peer(0))
    cross_near.start()

    for copy in scattered:
        copy.wait_recv()
    total = term[core, lo] + rs_buf[0] + rs_buf[1] + rs_buf[2]
    s_buf[core, lo] = total
    unit[...] = total.astype(BF16)

    landing = s.at[core, slab, y, h * 2 + lo]
    far_unit = remote(unit, landing, sc_tx.at[0], sc_rx.at[core], at_device(owner, to_z, y, 1 - h))
    near_unit = remote(unit, landing, sc_tx.at[1], sc_rx.at[core], at_device(owner, to_z, y, h))
    near_local = pltpu.make_async_copy(unit, landing, sc_rx.at[core])
    far_unit.start()

    @pl.when(stays)
    def _():
        near_local.start()

    @pl.when(jnp.logical_not(stays))
    def _():
        near_unit.start()

    groups = []
    for k in range(3):
        copy = remote(s_buf.at[core, lo], s_buf.at[core, lo], sg_tx.at[k], sg_rx.at[k], peer(k))
        copy.start()
        groups.append(copy)

    gathers = []
    slot = s.at[0, my_slab, y, my_piece]
    pltpu.make_async_copy(slot, slot, sc_rx.at[0]).wait()
    for k in range(1, ny):
        copy = remote(slot, slot, y_tx.at[k], y_rx.at[k], at_device(p, z, (y + k) % ny, h))
        copy.start()
        gathers.append(copy)
    slot = s.at[1, my_slab, y, my_piece]
    pltpu.make_async_copy(slot, slot, sc_rx.at[1]).wait()
    for k in range(1, nz):
        copy = remote(slot, slot, z_tx.at[k], z_rx.at[k], at_device(p, (z + k) % nz, y, h))
        copy.start()
        gathers.append(copy)

    cross_near.wait()
    cross_buf[...] = cross_buf[...] + cross[...]
    cross_twin = remote(cross_buf, cross_far, c_tx.at[1], c_rx.at[1], peer(1))
    cross_twin.start()
    base[...] = a[...].astype(F32).reshape(base.shape)
    hacc[...] = jnp.zeros_like(hacc)
    loads[3].wait()
    loads[4].wait()
    pltpu.make_async_copy(mine, cols, vc_rx).wait()
    second = dot(f[1], cols[1].reshape(width, panel).astype(F32), 1, 1, HIGH)
    at[1] = second.astype(BF16)
    first = dot(f[0], cols[0].reshape(width, panel).astype(F32), 1, 1, HIGH)

    def block(ring, place, part):
        if ring == 0:
            return 0, place // 4, pl.ds(part * (ny // 2), ny // 2), place % 4
        if depth > 1:
            return 1, pl.ds(part * (depth // 2), depth // 2), place, slice(None)
        return 1, 0, place, pl.ds(part * 2, 2)

    def ring_copy(ring, way, step, part):
        count, here = ((nz, z), (ny, y))[ring]
        sign = 1 - 2 * way
        place = (here - sign * (step - 1) + count) % count
        ahead = (here + sign + count) % count
        device = at_device(p, ahead, y, h) if ring == 0 else at_device(p, z, ahead, h)
        index = 2 * (step - 1) + (part if step < count // 2 else 0)
        where = s.at[block(ring, place, part)]
        return remote(where, where, ring_tx.at[ring, way, index], ring_rx.at[ring, way, index], device)

    def sent(ring, way, step, part):
        count = (nz, ny)[ring]
        return step < count // 2 or (step == count // 2 and part == way)

    for k in range(1, ny):
        where = s.at[0, my_slab, (y - k + ny) % ny, my_piece]
        remote(where, where, y_tx.at[k], y_rx.at[k], peer(0)).wait_recv()
    started = []
    for part in range(2):
        for way in range(2):
            if sent(0, way, 1, part):
                copy = ring_copy(0, way, 1, part)
                copy.start()
                started.append(copy)
    for k in range(1, nz):
        source = (z - k + nz) % nz
        where = s.at[1, source // 4, y, source % 4]
        remote(where, where, z_tx.at[k], z_rx.at[k], peer(0)).wait_recv()
    for part in range(2):
        for way in range(2):
            if sent(1, way, 1, part):
                copy = ring_copy(1, way, 1, part)
                copy.start()
                started.append(copy)

    cross_twin.wait()
    cross[...] = cross_buf[...] + cross_far[...]
    first = first - dot(f[0], dot(cross[...], second, 1, 0, HIGH), 1, 0, HIGH)
    at[0] = first.astype(BF16)

    def apply(ring, place, part):
        index = block(ring, place, part)
        tail = index[1:]
        values = s[index]
        lead = values.shape[:-1]
        count = values.size // panel
        piece = dot(values.reshape(count, panel), at[ring])
        base[tail] = base[tail] - piece.reshape(*lead, width)
        piece = piece.astype(BF16)
        for panel_id in range(2):
            vectors = v[(panel_id, *tail)].reshape(count, panel)
            hacc[panel_id] = hacc[panel_id] + dot(piece, vectors, 0, 0)

    for part in range(2):
        apply(0, z, part)
        apply(1, y, part)

    for step in range(1, max(nz, ny) // 2 + 1):
        for part in range(2):
            for ring in range(2):
                for way in range(2):
                    if not sent(ring, way, step, part):
                        continue
                    count, here = ((nz, z), (ny, y))[ring]
                    sign = 1 - 2 * way
                    place = (here - sign * step + count) % count
                    index = 2 * (step - 1) + (part if step < count // 2 else 0)
                    where = s.at[block(ring, place, part)]
                    remote(
                        where, where, ring_tx.at[ring, way, index], ring_rx.at[ring, way, index], peer(0)
                    ).wait_recv()
                    if sent(ring, way, step + 1, part):
                        copy = ring_copy(ring, way, step + 1, part)
                        copy.start()
                        started.append(copy)
                    apply(ring, place, part)

    near = remote(hacc, h_buf, h_tx.at[0], h_rx.at[0], peer(0))
    near.start()
    for copy in groups:
        copy.wait_send()
    for k in range(3):
        mate = mates[k]
        where = s_buf.at[mate % 2, mate // 2]
        remote(where, where, sg_tx.at[k], sg_rx.at[k], peer(k)).wait_recv()
    near.wait()
    chip = hacc[...] + h_buf[...]
    h_send[...] = chip.astype(BF16)
    twin = remote(h_send, h_far, h_tx.at[1], h_rx.at[1], peer(1))
    twin.start()
    twin.wait()
    rest = s_buf[...].reshape(2, width, panel) - chip - h_far[...].astype(F32)
    left_one = dot(rest[0], f[0], 1, 0, HIGH)
    left_two = dot(rest[1] - dot(left_one, cross[...], 1, 0, HIGH), f[1], 1, 0, HIGH)
    left_one = left_one.astype(BF16)
    left_two = left_two.astype(BF16)

    for slab_id in range(v.shape[1]):
        for column in range(ny):
            count = 4 * half_rows
            update = dot(v[0, slab_id, column].reshape(count, panel), left_one, 1, 1)
            update = update + dot(v[1, slab_id, column].reshape(count, panel), left_two, 1, 1)
            result = base[slab_id, column].reshape(count, width) - update
            out[pl.ds((slab_id * ny + column) * count, count)] = result.astype(BF16)

    for copy in scattered + gathers + started:
        copy.wait_send()
    far_unit.wait_send()

    @pl.when(jnp.logical_not(stays))
    def _():
        near_unit.wait_send()

    @pl.when(owner == p)
    def _():
        for copy in col_copies:
            copy.wait_send()


def body(parts, matrix, vectors_one, factor_one, vectors_two, factor_two):
    nz, ny, nh = parts
    depth = nz // ROWS
    rows, width = matrix.shape
    panel = factor_one.shape[0]
    half = width // 2
    grid = (depth, ny, 4, half)
    hbm = pl.BlockSpec(memory_space=pl.ANY)
    dma = pltpu.SemaphoreType.DMA
    most = max(nz, ny)
    flops = 2 * rows * width * panel * 10
    return pl.pallas_call(
        functools.partial(kernel, parts),
        out_shape=jax.ShapeDtypeStruct((rows, width), BF16),
        in_specs=[hbm] * 5,
        out_specs=pl.BlockSpec(memory_space=pltpu.VMEM),
        scratch_shapes=[
            pltpu.VMEM((rows, width), BF16),
            pltpu.VMEM((2, *grid, panel), BF16),
            pltpu.VMEM((2, panel, panel), F32),
            pltpu.VMEM((2, 2, half, panel), F32),
            pltpu.VMEM((3, half, panel), F32),
            pltpu.VMEM((2, 2, half, panel), F32),
            pltpu.VMEM((half, panel), BF16),
            pltpu.VMEM((2, *grid, panel), BF16),
            pltpu.VMEM((2, 2, half, panel), BF16),
            pltpu.VMEM((panel, panel), F32),
            pltpu.VMEM((panel, panel), F32),
            pltpu.VMEM((panel, panel), F32),
            pltpu.VMEM((2, panel, width), BF16),
            pltpu.VMEM((*grid, width), F32),
            pltpu.VMEM((2, width, panel), F32),
            pltpu.VMEM((2, width, panel), F32),
            pltpu.VMEM((2, width, panel), BF16),
            pltpu.VMEM((2, width, panel), BF16),
            dma((5,)),
            dma((3,)),
            dma((3,)),
            dma((3,)),
            dma,
            dma((3,)),
            dma((3,)),
            dma((2,)),
            dma((2,)),
            dma((2,)),
            dma((2,)),
            dma((2,)),
            dma((2,)),
            dma((ny,)),
            dma((ny,)),
            dma((nz,)),
            dma((nz,)),
            dma((2, 2, most)),
            dma((2, 2, most)),
        ],
        compiler_params=pltpu.CompilerParams(
            collective_id=0, has_side_effects=True, vmem_limit_bytes=40 * 1024 * 1024
        ),
        cost_estimate=pl.CostEstimate(flops=flops, bytes_accessed=4 * rows * panel, transcendentals=0),
    )(
        matrix,
        vectors_one.reshape(*grid, panel),
        vectors_two.reshape(*grid, panel),
        factor_one,
        factor_two,
    )


def build(mesh, parts):
    placed = (P("prow", "pcol"), P("prow", None), P(), P("prow", None), P())
    return jax.shard_map(
        functools.partial(body, parts), mesh=mesh, in_specs=placed, out_specs=P("prow", "pcol"), check_vma=False
    )


def solution(mesh):
    return build(mesh, PARTS)
```

```python
import functools

import jax
import jax.numpy as jnp
from jax import lax
from jax.experimental import pallas as pl
from jax.experimental.pallas import tpu as pltpu
from jax.sharding import PartitionSpec as P

MESH = pl.DeviceIdType.MESH
HIGH = lax.Precision.HIGHEST
PARTS = (8, 8, 2)
ROWS = 4
F32 = jnp.float32
BF16 = jnp.bfloat16


def dot(lhs, rhs, left=1, right=0, precision=None):
    return lax.dot_general(
        lhs, rhs, (((left,), (right,)), ((), ())), precision=precision, preferred_element_type=F32
    )


def kernel(
    parts,
    a_hbm, v1_hbm, v2_hbm, f1_hbm, f2_hbm,
    out,
    a, v, f, term, rs_buf, s_buf, unit, s, cols, cross, cross_buf, cross_far, at, base, hacc, h_buf, h_send, h_far,
    load, f_load, rs_tx, rs_rx, vc_tx, vc_rx, sg_tx, sg_rx, sc_tx, sc_rx, c_tx, c_rx, h_tx, h_rx,
    first_tx, first_rx, ring_tx, ring_rx,
):
    nz, ny, nh = parts
    depth = nz // ROWS
    half_rows, panel = unit.shape
    width = 2 * half_rows
    run = 4 * half_rows
    p = lax.axis_index("prow")
    q = lax.axis_index("pcol")
    z, y, h = q // (ny * nh), (q // nh) % ny, q % nh
    lo, core = p // 2, p % 2
    mates = (2 * lo + 1 - core, 2 * (1 - lo) + core, 3 - p)

    def at_device(row, zi, yi, hi):
        return {"prow": row, "pcol": (zi * ny + yi) * nh + hi}

    def peer(k):
        return {"prow": mates[k], "pcol": q}

    def remote(src, dst, tx, rx, device):
        return pltpu.make_async_remote_copy(
            src_ref=src, dst_ref=dst, send_sem=tx, recv_sem=rx, device_id=device, device_id_type=MESH
        )

    later = []

    def send(copy):
        copy.start()
        later.append(copy.wait_send)

    owner, slab = z // depth, z % depth
    counts, heres = (nz, ny), (z, y)

    def along(ring, place):
        return at_device(p, place, y, h) if ring == 0 else at_device(p, z, place, h)

    number = (slab * 4) + 2 * h + lo
    to = jnp.where(core == 0, y, number), jnp.where(core == 0, number, y)
    stays = (owner == p) & (to[0] == z) & (to[1] == y)

    def origin(k):
        place, unit_number = ((z, y), (y, z))[k]
        piece = unit_number % 4
        return 2 * (piece % 2) + k, p * depth + unit_number // 4, place, piece // 2

    halves = [(k, part) for part in range(depth) for k in range(2)]
    loads = [pltpu.make_async_copy(a_hbm, a, load.at[0])]
    for place, (k, part) in enumerate(halves):
        loads.append(pltpu.make_async_copy((v1_hbm, v2_hbm)[k].at[part], v.at[k, part], load.at[1 + place]))
    for copy in loads:
        copy.start()
    factors = [pltpu.make_async_copy((f1_hbm, f2_hbm)[k], f.at[k], f_load.at[k]) for k in range(2)]
    for copy in factors:
        copy.start()

    barrier = pltpu.get_barrier_semaphore()

    def greet(device):
        pl.semaphore_signal(barrier, inc=1, device_id=device, device_id_type=MESH)

    for k in range(3):
        greet(peer(k))
    for ring in range(2):
        for k in range(1, counts[ring]):
            greet(along(ring, (heres[ring] + k) % counts[ring]))
    for k in range(2):
        from_p, from_z, from_y, from_h = origin(k)

        @pl.when(jnp.logical_not((from_p == p) & (from_z == z) & (from_y == y) & (from_h == h)))
        def _():
            greet(at_device(from_p, from_z, from_y, from_h))

    stretch = ny * run
    sums = [None, None]
    loads[0].wait()
    for place, (k, part) in enumerate(halves):
        loads[1 + place].wait()
        more = dot(a[:, part * stretch : (part + 1) * stretch], v[k, part].reshape(stretch, panel))
        sums[k] = more if sums[k] is None else sums[k] + more
    for k in range(2):
        term[k] = sums[k].reshape(2, half_rows, panel)

    pl.semaphore_wait(barrier, 3 + (ny - 1) + (nz - 1) + 2 - jnp.where(stays, 1, 0))

    scattered = []
    for k in (2, 1, 0):
        mate = mates[k]
        copy = remote(term.at[mate % 2, mate // 2], rs_buf.at[k], rs_tx.at[k], rs_rx.at[k], peer(k))
        send(copy)
        scattered.append(copy)

    rows = depth * stretch
    cross[...] = dot(v[0].reshape(rows, panel), v[1].reshape(rows, panel), 0, 0)

    for copy in scattered:
        copy.wait_recv()
    total = term[core, lo] + rs_buf[0] + rs_buf[1] + rs_buf[2]
    unit[...] = total.astype(BF16)
    s_buf[core, lo] = total

    landing = s.at[core, slab, y, pl.ds((2 * h + lo) * half_rows, half_rows)]
    far_unit = remote(unit, landing, sc_tx.at[0], sc_rx.at[core], at_device(owner, to[0], to[1], 1 - h))
    near_unit = remote(unit, landing, sc_tx.at[1], sc_rx.at[core], at_device(owner, to[0], to[1], h))
    near_local = pltpu.make_async_copy(unit, landing, sc_rx.at[core])
    send(far_unit)

    @pl.when(stays)
    def _():
        near_local.start()

    @pl.when(jnp.logical_not(stays))
    def _():
        near_unit.start()

    def near_sent():
        @pl.when(jnp.logical_not(stays))
        def _():
            near_unit.wait_send()

    later.append(near_sent)

    def first_slot(k, unit_number):
        piece = pl.multiple_of(unit_number % 4 * half_rows, half_rows)
        return s.at[k, unit_number // 4, heres[k], pl.ds(piece, half_rows)]

    for k in range(2):
        slot = first_slot(k, heres[1 - k])
        pltpu.make_async_copy(slot, slot, sc_rx.at[k]).wait()
        count = counts[1 - k]
        for j in range(1, count):
            send(remote(slot, slot, first_tx.at[k, j], first_rx.at[k, j], along(1 - k, (heres[1 - k] + j) % count)))

    for k in range(3):
        send(remote(s_buf.at[core, lo], s_buf.at[core, lo], sg_tx.at[k], sg_rx.at[k], peer(k)))
    mine = v.at[:, slab, y, pl.ds(pl.multiple_of(2 * h * half_rows, half_rows), width)]
    col_copies = [remote(mine, cols, vc_tx.at[k], vc_rx, peer(k)) for k in range(3)]
    col_local = pltpu.make_async_copy(mine, cols, vc_rx)

    @pl.when(owner == p)
    def _():
        for copy in col_copies:
            copy.start()
        col_local.start()

    def cols_sent():
        @pl.when(owner == p)
        def _():
            for copy in col_copies:
                copy.wait_send()

    later.append(cols_sent)
    cross_near = remote(cross, cross_buf, c_tx.at[0], c_rx.at[0], peer(0))
    cross_near.start()
    hacc[...] = jnp.zeros_like(hacc)
    base[...] = jnp.zeros_like(base)
    cross_near.wait()
    cross_buf[...] = cross_buf[...] + cross[...]
    cross_twin = remote(cross_buf, cross_far, c_tx.at[1], c_rx.at[1], peer(1))
    cross_twin.start()
    for copy in factors:
        copy.wait()

    def sums_here():
        for k in range(3):
            mate = mates[k]
            where = s_buf.at[mate % 2, mate // 2]
            remote(where, where, sg_tx.at[k], sg_rx.at[k], peer(k)).wait_recv()

    def firsts_here(k):
        count = counts[1 - k]
        for j in range(1, count):
            where = first_slot(k, (heres[1 - k] - j + count) % count)
            remote(where, where, first_tx.at[k, j], first_rx.at[k, j], peer(0)).wait_recv()

    def cols_here():
        pltpu.make_async_copy(mine, cols, vc_rx).wait()


    def block(ring, place, part):
        if depth > 1:
            return s.at[ring, part, place]
        return s.at[ring, 0, place, pl.ds(part * (run // 2), run // 2)]

    def sent(ring, way, step, part):
        half_way = counts[ring] // 2
        return step < half_way or (step == half_way and part == way)

    def ring_copy(ring, way, step, part, receiving=False):
        count, here, sign = counts[ring], heres[ring], 1 - 2 * way
        place = (here - sign * (step if receiving else step - 1) + count) % count
        index = 2 * (step - 1) + (part if step < count // 2 else 0)
        where = block(ring, place, part)
        sems = ring_tx.at[ring, way, index], ring_rx.at[ring, way, index]
        return remote(where, where, *sems, along(ring, (here + sign + count) % count))

    for ring in range(2):
        firsts_here(ring)
        for part in range(2):
            for way in range(2):
                if sent(ring, way, 1, part):
                    send(ring_copy(ring, way, 1, part))

    cols_here()
    second = dot(cols[1].astype(F32), f[1], 1, 1, HIGH)
    at[1] = second.astype(BF16)
    cross_twin.wait()
    cross[...] = cross_buf[...] + cross_far[...]
    first = dot(cols[0].astype(F32) - dot(second, cross[...], 1, 1, HIGH), f[0], 1, 1, HIGH)
    at[0] = first.astype(BF16)

    def apply(ring, place, part):
        if depth > 1:
            tail = (part, place)
        else:
            tail = (0, place, slice(part * (run // 2), (part + 1) * (run // 2)))
        piece = dot(at[ring], s[(ring, *tail)], 1, 1)
        if depth > 1:
            base[part, place] = base[part, place] + piece
        else:
            base[0, place, :, tail[2]] = base[0, place, :, tail[2]] + piece
        piece = piece.astype(BF16)
        for k in range(2):
            hacc[k] = hacc[k] + dot(piece, v[(k, *tail)])

    for part in range(2):
        for ring in range(2):
            apply(ring, heres[ring], part)

    for step in range(1, max(nz, ny) // 2 + 1):
        for part in range(2):
            for ring in range(2):
                for way in range(2):
                    if not sent(ring, way, step, part):
                        continue
                    ring_copy(ring, way, step, part, receiving=True).wait_recv()
                    if sent(ring, way, step + 1, part):
                        send(ring_copy(ring, way, step + 1, part))
                    count, here, sign = counts[ring], heres[ring], 1 - 2 * way
                    apply(ring, (here - sign * step + count) % count, part)

    sums_here()
    near = remote(hacc, h_buf, h_tx.at[0], h_rx.at[0], peer(0))
    near.start()
    near.wait()
    chip = hacc[...] + h_buf[...]
    h_send[...] = chip.astype(BF16)
    twin = remote(h_send, h_far, h_tx.at[1], h_rx.at[1], peer(1))
    twin.start()
    rest = s_buf[...].reshape(2, width, panel) - chip
    twin.wait()
    rest = rest - h_far[...].astype(F32)
    left_one = dot(rest[0], f[0], 1, 0, HIGH)
    left_two = dot(rest[1] - dot(left_one, cross[...], 1, 0, HIGH), f[1], 1, 0, HIGH)
    left = left_one.astype(BF16), left_two.astype(BF16)

    for part in range(depth):
        for place in range(0, ny, 2):
            spot = slice((part * ny + place) * run, (part * ny + place + 2) * run)
            pair = slice(place, place + 2)
            update = jnp.concatenate([base[part, place], base[part, place + 1]], axis=1)
            for k in range(2):
                update = update + dot(left[k], v[k, part, pair].reshape(2 * run, panel), 1, 1)
            out[:, spot] = (a[:, spot].astype(F32) - update).astype(BF16)

    for wait in later:
        wait()


def body(parts, matrix, vectors_one, factor_one, vectors_two, factor_two):
    nz, ny, nh = parts
    depth = nz // ROWS
    rows, width = matrix.shape
    panel = factor_one.shape[0]
    half = width // 2
    grid = (depth, ny, 4 * half)
    hbm = pl.BlockSpec(memory_space=pltpu.HBM)
    dma = pltpu.SemaphoreType.DMA
    most = max(nz, ny)
    flops = 2 * rows * width * panel * 10
    result = pl.pallas_call(
        functools.partial(kernel, parts),
        out_shape=jax.ShapeDtypeStruct((width, rows), BF16),
        in_specs=[hbm] * 5,
        out_specs=pl.BlockSpec(memory_space=pltpu.VMEM),
        scratch_shapes=[
            pltpu.VMEM((width, rows), BF16),
            pltpu.VMEM((2, *grid, panel), BF16),
            pltpu.VMEM((2, panel, panel), F32),
            pltpu.VMEM((2, 2, half, panel), F32),
            pltpu.VMEM((3, half, panel), F32),
            pltpu.VMEM((2, 2, half, panel), F32),
            pltpu.VMEM((half, panel), BF16),
            pltpu.VMEM((2, *grid, panel), BF16),
            pltpu.VMEM((2, width, panel), BF16),
            pltpu.VMEM((panel, panel), F32),
            pltpu.VMEM((panel, panel), F32),
            pltpu.VMEM((panel, panel), F32),
            pltpu.VMEM((2, width, panel), BF16),
            pltpu.VMEM((depth, ny, width, 4 * half), F32),
            pltpu.VMEM((2, width, panel), F32),
            pltpu.VMEM((2, width, panel), F32),
            pltpu.VMEM((2, width, panel), BF16),
            pltpu.VMEM((2, width, panel), BF16),
            dma((1 + 2 * depth,)),
            dma((2,)),
            dma((3,)),
            dma((3,)),
            dma((3,)),
            dma,
            dma((3,)),
            dma((3,)),
            dma((2,)),
            dma((2,)),
            dma((2,)),
            dma((2,)),
            dma((2,)),
            dma((2,)),
            dma((2, most)),
            dma((2, most)),
            dma((2, 2, most)),
            dma((2, 2, most)),
        ],
        compiler_params=pltpu.CompilerParams(
            collective_id=0, has_side_effects=True, vmem_limit_bytes=56 * 1024 * 1024
        ),
        cost_estimate=pl.CostEstimate(flops=flops, bytes_accessed=4 * rows * panel, transcendentals=0),
    )(matrix.T, vectors_one.reshape(*grid, panel), vectors_two.reshape(*grid, panel), factor_one, factor_two)
    return result.T


def build(mesh, parts):
    placed = (P("prow", "pcol"), P("prow", None), P(), P("prow", None), P())
    return jax.shard_map(
        functools.partial(body, parts), mesh=mesh, in_specs=placed, out_specs=P("prow", "pcol"), check_vma=False
    )


def solution(mesh):
    return build(mesh, PARTS)
```

```python
import functools

import jax
import jax.numpy as jnp
from jax import lax
from jax.experimental import pallas as pl
from jax.experimental.pallas import tpu as pltpu
from jax.sharding import PartitionSpec as P

MESH = pl.DeviceIdType.MESH
HIGH = lax.Precision.HIGHEST
PARTS = (8, 8, 2)
ROWS = 4
F32 = jnp.float32
BF16 = jnp.bfloat16


def dot(lhs, rhs, left=1, right=0, precision=None):
    return lax.dot_general(
        lhs, rhs, (((left,), (right,)), ((), ())), precision=precision, preferred_element_type=F32
    )


def kernel(
    parts,
    a_hbm, v1_hbm, v2_hbm, f1_hbm, f2_hbm,
    out,
    a, v, f, term, rs_buf, s_buf, unit, s, cols, cross, cross_buf, cross_far, at, base, hacc, h_buf, h_send, h_far,
    load, f_load, rs_tx, rs_rx, vc_tx, vc_rx, sg_tx, sg_rx, sc_tx, sc_rx, c_tx, c_rx, h_tx, h_rx,
    first_tx, first_rx, ring_tx, ring_rx,
):
    nz, ny, nh = parts
    depth = nz // ROWS
    half_rows, panel = unit.shape
    width = 2 * half_rows
    run = 4 * half_rows
    p = lax.axis_index("prow")
    q = lax.axis_index("pcol")
    z, y, h = q // (ny * nh), (q // nh) % ny, q % nh
    lo, core = p // 2, p % 2
    mates = (2 * lo + 1 - core, 2 * (1 - lo) + core, 3 - p)

    def at_device(row, zi, yi, hi):
        return {"prow": row, "pcol": (zi * ny + yi) * nh + hi}

    def peer(k):
        return {"prow": mates[k], "pcol": q}

    def remote(src, dst, tx, rx, device):
        return pltpu.make_async_remote_copy(
            src_ref=src, dst_ref=dst, send_sem=tx, recv_sem=rx, device_id=device, device_id_type=MESH
        )

    later = []

    def send(copy):
        copy.start()
        later.append(copy.wait_send)

    owner, slab = z // depth, z % depth
    counts, heres = (nz, ny), (z, y)

    def along(ring, place):
        return at_device(p, place, y, h) if ring == 0 else at_device(p, z, place, h)

    number = slab * 4 + 2 * h + lo
    stays = (owner == p) & (number == z)
    from_z, from_h, from_lo = p * depth + z // 4, z % 4 // 2, z % 2

    halves = [(k, part) for part in range(depth) for k in range(2)]
    loads = [pltpu.make_async_copy(a_hbm, a, load.at[0])]
    for place, (k, part) in enumerate(halves):
        loads.append(pltpu.make_async_copy((v1_hbm, v2_hbm)[k].at[part], v.at[k, part], load.at[1 + place]))
    for copy in loads:
        copy.start()
    factors = [pltpu.make_async_copy((f1_hbm, f2_hbm)[k], f.at[k], f_load.at[k]) for k in range(2)]
    for copy in factors:
        copy.start()

    barrier = pltpu.get_barrier_semaphore()

    def greet(device):
        pl.semaphore_signal(barrier, inc=1, device_id=device, device_id_type=MESH)

    for k in range(3):
        greet(peer(k))
    for ring in range(2):
        for k in range(1, counts[ring]):
            greet(along(ring, (heres[ring] + k) % counts[ring]))
    for k in range(2):
        from_p = 2 * from_lo + k

        @pl.when(jnp.logical_not((from_p == p) & (from_z == z) & (from_h == h)))
        def _():
            greet(at_device(from_p, from_z, y, from_h))

    stretch = ny * run
    sums = [None, None]
    loads[0].wait()
    for place, (k, part) in enumerate(halves):
        loads[1 + place].wait()
        more = dot(a[:, part * stretch : (part + 1) * stretch], v[k, part].reshape(stretch, panel))
        sums[k] = more if sums[k] is None else sums[k] + more
    for k in range(2):
        term[k] = sums[k].reshape(2, half_rows, panel)

    pl.semaphore_wait(barrier, 3 + (ny - 1) + (nz - 1) + 2 - jnp.where(stays, 1, 0))

    scattered = []
    for k in (2, 1, 0):
        mate = mates[k]
        copy = remote(term.at[mate % 2, mate // 2], rs_buf.at[k], rs_tx.at[k], rs_rx.at[k], peer(k))
        send(copy)
        scattered.append(copy)

    rows = depth * stretch
    cross[...] = dot(v[0].reshape(rows, panel), v[1].reshape(rows, panel), 0, 0)
    cross_near = remote(cross, cross_buf, c_tx.at[0], c_rx.at[0], peer(0))
    cross_near.start()

    for copy in scattered:
        copy.wait_recv()
    total = term[core, lo] + rs_buf[0] + rs_buf[1] + rs_buf[2]
    unit[...] = total.astype(BF16)

    landing = s.at[core, slab, y, pl.ds((2 * h + lo) * half_rows, half_rows)]
    far_unit = remote(unit, landing, sc_tx.at[0], sc_rx.at[core], at_device(owner, number, y, 1 - h))
    near_unit = remote(unit, landing, sc_tx.at[1], sc_rx.at[core], at_device(owner, number, y, h))
    near_local = pltpu.make_async_copy(unit, landing, sc_rx.at[core])
    send(far_unit)

    @pl.when(stays)
    def _():
        near_local.start()

    @pl.when(jnp.logical_not(stays))
    def _():
        near_unit.start()

    def near_sent():
        @pl.when(jnp.logical_not(stays))
        def _():
            near_unit.wait_send()

    later.append(near_sent)

    s_buf[core, lo] = total

    def units(ring, place, spot, pair):
        if ring == 0:
            piece = pl.ds(pl.multiple_of(place % 4 * half_rows, half_rows), half_rows)
            return s.at[0, place // 4, pl.ds(2 * spot, 2) if pair else spot, piece]
        if pair:
            return s.at[1, spot // 2, place, pl.ds(pl.multiple_of(spot % 2 * width, width), width)]
        return s.at[1, spot // 4, place, pl.ds(pl.multiple_of(spot % 4 * half_rows, half_rows), half_rows)]

    for ring in range(2):
        slot = units(ring, heres[ring], heres[1 - ring], False)
        pltpu.make_async_copy(slot, slot, sc_rx.at[ring]).wait()
        count = counts[1 - ring]
        for j in sorted(range(1, count), key=lambda j: min(j, count - j)):
            device = along(1 - ring, (heres[1 - ring] + j) % count)
            send(remote(slot, slot, first_tx.at[ring, j], first_rx.at[ring, j], device))

    for k in range(3):
        send(remote(s_buf.at[core, lo], s_buf.at[core, lo], sg_tx.at[k], sg_rx.at[k], peer(k)))
    mine = v.at[:, slab, y, pl.ds(pl.multiple_of(2 * h * half_rows, half_rows), width)]
    col_copies = [remote(mine, cols, vc_tx.at[k], vc_rx, peer(k)) for k in range(3)]
    col_local = pltpu.make_async_copy(mine, cols, vc_rx)

    @pl.when(owner == p)
    def _():
        for copy in col_copies:
            copy.start()
        col_local.start()

    def cols_sent():
        @pl.when(owner == p)
        def _():
            for copy in col_copies:
                copy.wait_send()

    later.append(cols_sent)
    hacc[...] = jnp.zeros_like(hacc)
    cross_near.wait()
    cross_buf[...] = cross_buf[...] + cross[...]
    cross_twin = remote(cross_buf, cross_far, c_tx.at[1], c_rx.at[1], peer(1))
    cross_twin.start()

    def pairs(ring):
        count = counts[1 - ring] // 2
        return [0] + [k for d in range(1, count) for k in (d, -d) if d < count - d or (d == count - d and k > 0)]

    def sent(ring, way, step, j):
        half_way, many = counts[ring] // 2, counts[1 - ring] // 2
        return step < half_way or (step == half_way and j * 2 // many == way)

    def pair_at(ring, j):
        many = counts[1 - ring] // 2
        return (heres[1 - ring] // 2 + pairs(ring)[j] + many) % many

    def ring_copy(ring, way, step, j, receiving=False):
        count, here, sign = counts[ring], heres[ring], 1 - 2 * way
        place = (here - sign * (step if receiving else step - 1) + count) % count
        index = (step - 1) * (counts[1 - ring] // 2) + j
        where = units(ring, place, pair_at(ring, j), True)
        sems = ring_tx.at[ring, way, index], ring_rx.at[ring, way, index]
        return remote(where, where, *sems, along(ring, (here + sign + count) % count))

    for j in range(max(nz, ny) // 2):
        for ring in range(2):
            count, here = counts[1 - ring], heres[1 - ring]
            if j >= count // 2:
                continue
            for spot in [2 * pair_at(ring, j), 2 * pair_at(ring, j) + 1] if j else [here // 2 * 2 + 1 - here % 2]:
                where = units(ring, heres[ring], spot, False)
                k = (here - spot + count) % count
                remote(where, where, first_tx.at[ring, k], first_rx.at[ring, k], peer(0)).wait_recv()
            for way in range(2):
                send(ring_copy(ring, way, 1, j))

    for copy in factors:
        copy.wait()
    pltpu.make_async_copy(mine, cols, vc_rx).wait()
    second = dot(cols[1].astype(F32), f[1], 1, 1, HIGH)
    at[1] = second.astype(BF16)
    cross_twin.wait()
    cross[...] = cross_buf[...] + cross_far[...]
    first = dot(cols[0].astype(F32) - dot(second, cross[...], 1, 1, HIGH), f[0], 1, 1, HIGH)
    at[0] = first.astype(BF16)

    def apply(ring, place):
        if ring == 0:
            tail = (place // 4, slice(None), pl.ds(pl.multiple_of(place % 4 * half_rows, half_rows), half_rows))
            many = ny * half_rows
        else:
            tail = (slice(None), place)
            many = depth * run
        piece = dot(at[ring], s[(ring, *tail)].reshape(many, panel), 1, 1).astype(BF16)
        for k in range(2):
            hacc[k] = hacc[k] + dot(piece, v[(k, *tail)].reshape(many, panel))

    for ring in range(2):
        apply(ring, heres[ring])

    for step in range(1, max(nz, ny) // 2 + 1):
        for j in range(max(nz, ny) // 2):
            for ring in range(2):
                if j >= counts[1 - ring] // 2:
                    continue
                for way in range(2):
                    if not sent(ring, way, step, j):
                        continue
                    ring_copy(ring, way, step, j, receiving=True).wait_recv()
                    if sent(ring, way, step + 1, j):
                        send(ring_copy(ring, way, step + 1, j))
        for ring in range(2):
            count, here = counts[ring], heres[ring]
            for place in (here - step + count, here + step)[: 2 if step < count // 2 else 1]:
                if step <= count // 2:
                    apply(ring, place % count)

    near = remote(hacc, h_buf, h_tx.at[0], h_rx.at[0], peer(0))
    near.start()
    pairs_of_places = [(part, place) for part in range(depth) for place in range(0, ny, 2)]

    def right(part, place):
        spot = slice((part * ny + place) * run, (part * ny + place + 2) * run)
        update = dot(at[0], s[0, part, place : place + 2].reshape(2 * run, panel), 1, 1)
        update = update + dot(at[1], s[1, part, place : place + 2].reshape(2 * run, panel), 1, 1)
        base[:, spot] = a[:, spot].astype(F32) - update

    near.wait()
    chip = hacc[...] + h_buf[...]
    h_send[...] = chip.astype(BF16)
    twin = remote(h_send, h_far, h_tx.at[1], h_rx.at[1], peer(1))
    twin.start()
    for part, place in pairs_of_places:
        right(part, place)
    for k in range(3):
        mate = mates[k]
        where = s_buf.at[mate % 2, mate // 2]
        remote(where, where, sg_tx.at[k], sg_rx.at[k], peer(k)).wait_recv()
    rest = s_buf[...].reshape(2, width, panel) - chip
    twin.wait()
    rest = rest - h_far[...].astype(F32)
    left_one = dot(rest[0], f[0], 1, 0, HIGH)
    left_two = dot(rest[1] - dot(left_one, cross[...], 1, 0, HIGH), f[1], 1, 0, HIGH)
    left = left_one.astype(BF16), left_two.astype(BF16)

    for part, place in pairs_of_places:
        spot = slice((part * ny + place) * run, (part * ny + place + 2) * run)
        update = dot(left[0], v[0, part, place : place + 2].reshape(2 * run, panel), 1, 1)
        update = update + dot(left[1], v[1, part, place : place + 2].reshape(2 * run, panel), 1, 1)
        out[:, spot] = (base[:, spot] - update).astype(BF16)

    for wait in later:
        wait()


def body(parts, matrix, vectors_one, factor_one, vectors_two, factor_two):
    nz, ny, nh = parts
    depth = nz // ROWS
    rows, width = matrix.shape
    panel = factor_one.shape[0]
    half = width // 2
    grid = (depth, ny, 4 * half)
    hbm = pl.BlockSpec(memory_space=pltpu.HBM)
    dma = pltpu.SemaphoreType.DMA
    most = max(nz, ny)
    flops = 2 * rows * width * panel * 10
    result = pl.pallas_call(
        functools.partial(kernel, parts),
        out_shape=pltpu.VMEM((width, rows), BF16),
        in_specs=[hbm] * 5,
        out_specs=pl.BlockSpec(memory_space=pltpu.VMEM),
        scratch_shapes=[
            pltpu.VMEM((width, rows), BF16),
            pltpu.VMEM((2, *grid, panel), BF16),
            pltpu.VMEM((2, panel, panel), F32),
            pltpu.VMEM((2, 2, half, panel), F32),
            pltpu.VMEM((3, half, panel), F32),
            pltpu.VMEM((2, 2, half, panel), F32),
            pltpu.VMEM((half, panel), BF16),
            pltpu.VMEM((2, *grid, panel), BF16),
            pltpu.VMEM((2, width, panel), BF16),
            pltpu.VMEM((panel, panel), F32),
            pltpu.VMEM((panel, panel), F32),
            pltpu.VMEM((panel, panel), F32),
            pltpu.VMEM((2, width, panel), BF16),
            pltpu.VMEM((width, rows), F32),
            pltpu.VMEM((2, width, panel), F32),
            pltpu.VMEM((2, width, panel), F32),
            pltpu.VMEM((2, width, panel), BF16),
            pltpu.VMEM((2, width, panel), BF16),
            dma((1 + 2 * depth,)),
            dma((2,)),
            dma((3,)),
            dma((3,)),
            dma((3,)),
            dma,
            dma((3,)),
            dma((3,)),
            dma((2,)),
            dma((2,)),
            dma((2,)),
            dma((2,)),
            dma((2,)),
            dma((2,)),
            dma((2, most)),
            dma((2, most)),
            dma((2, 2, most * most // 4)),
            dma((2, 2, most * most // 4)),
        ],
        compiler_params=pltpu.CompilerParams(
            collective_id=0, has_side_effects=True, vmem_limit_bytes=56 * 1024 * 1024
        ),
        cost_estimate=pl.CostEstimate(flops=flops, bytes_accessed=4 * rows * panel, transcendentals=0),
    )(matrix.T, vectors_one.reshape(*grid, panel), vectors_two.reshape(*grid, panel), factor_one, factor_two)
    return result.T


def build(mesh, parts):
    placed = (P("prow", "pcol"), P("prow", None), P(), P("prow", None), P())
    return jax.shard_map(
        functools.partial(body, parts), mesh=mesh, in_specs=placed, out_specs=P("prow", "pcol"), check_vma=False
    )


def solution(mesh):
    return build(mesh, PARTS)
```

```python
import functools

import jax
import jax.numpy as jnp
from jax import lax
from jax.experimental import pallas as pl
from jax.experimental.pallas import tpu as pltpu
from jax.sharding import PartitionSpec as P

MESH = pl.DeviceIdType.MESH
HIGH = lax.Precision.HIGHEST
PARTS = (8, 8, 2)
ROWS = 4
F32 = jnp.float32
BF16 = jnp.bfloat16


def dot(lhs, rhs, left=1, right=0, precision=None):
    return lax.dot_general(
        lhs, rhs, (((left,), (right,)), ((), ())), precision=precision, preferred_element_type=F32
    )


def kernel(
    parts,
    a_hbm, v1_hbm, v2_hbm, f1_hbm, f2_hbm,
    out,
    a, v, f, mix, split, h_near, term, term_send, rs_buf, s_buf, unit, s, cols, cross, cross_buf, cross_far, at, base, hacc, h_buf, h_send, h_far,
    load, f_load, rs_tx, rs_rx, vc_tx, vc_rx, sg_tx, sg_rx, sc_tx, sc_rx, c_tx, c_rx, h_tx, h_rx,
    first_tx, first_rx, ring_tx, ring_rx,
):
    nz, ny, nh = parts
    depth = nz // ROWS
    half_rows, panel = unit.shape
    width = 2 * half_rows
    run = 4 * half_rows
    p = lax.axis_index("prow")
    q = lax.axis_index("pcol")
    z, y, h = q // (ny * nh), (q // nh) % ny, q % nh
    lo, core = p // 2, p % 2
    mates = (2 * lo + 1 - core, 2 * (1 - lo) + core, 3 - p)

    def at_device(row, zi, yi, hi):
        return {"prow": row, "pcol": (zi * ny + yi) * nh + hi}

    def peer(k):
        return {"prow": mates[k], "pcol": q}

    def remote(src, dst, tx, rx, device):
        return pltpu.make_async_remote_copy(
            src_ref=src, dst_ref=dst, send_sem=tx, recv_sem=rx, device_id=device, device_id_type=MESH
        )

    later = []

    def send(copy):
        copy.start()
        later.append(copy.wait_send)

    owner, slab = z // depth, z % depth
    counts, heres = (nz, ny), (z, y)

    def along(ring, place):
        return at_device(p, place, y, h) if ring == 0 else at_device(p, z, place, h)

    number = slab * 4 + 2 * h + lo
    stays = (owner == p) & (number == z)
    from_z, from_h, from_lo = p * depth + z // 4, z % 4 // 2, z % 2

    halves = [(k, part) for part in range(depth) for k in range(2)]
    loads = [pltpu.make_async_copy(a_hbm, a, load.at[0])]
    for place, (k, part) in enumerate(halves):
        loads.append(pltpu.make_async_copy((v1_hbm, v2_hbm)[k].at[part], v.at[k, part], load.at[1 + place]))
    for copy in loads:
        copy.start()
    factors = [pltpu.make_async_copy((f1_hbm, f2_hbm)[k], f.at[k], f_load.at[k]) for k in range(2)]
    for copy in factors:
        copy.start()

    barrier = pltpu.get_barrier_semaphore()

    def greet(device):
        pl.semaphore_signal(barrier, inc=1, device_id=device, device_id_type=MESH)

    for k in range(3):
        greet(peer(k))
    for ring in range(2):
        for k in range(1, counts[ring]):
            greet(along(ring, (heres[ring] + k) % counts[ring]))
    for k in range(2):
        from_p = 2 * from_lo + k

        @pl.when(jnp.logical_not((from_p == p) & (from_z == z) & (from_h == h)))
        def _():
            greet(at_device(from_p, from_z, y, from_h))

    stretch = ny * run
    sums = [None, None]
    loads[0].wait()
    for place, (k, part) in enumerate(halves):
        loads[1 + place].wait()
        more = dot(a[:, part * stretch : (part + 1) * stretch], v[k, part].reshape(stretch, panel))
        sums[k] = more if sums[k] is None else sums[k] + more
    for k in range(2):
        term[k] = sums[k].reshape(2, half_rows, panel)
        term_send[k] = sums[k].reshape(2, half_rows, panel).astype(BF16)

    pl.semaphore_wait(barrier, 3 + (ny - 1) + (nz - 1) + 2 - jnp.where(stays, 1, 0))

    scattered = []
    for k in (2, 1, 0):
        mate = mates[k]
        copy = remote(term_send.at[mate % 2, mate // 2], rs_buf.at[k], rs_tx.at[k], rs_rx.at[k], peer(k))
        send(copy)
        scattered.append(copy)

    rows = depth * stretch
    cross[...] = dot(v[0].reshape(rows, panel), v[1].reshape(rows, panel), 0, 0)
    cross_near = remote(cross, cross_buf, c_tx.at[0], c_rx.at[0], peer(0))
    cross_near.start()

    for copy in scattered:
        copy.wait_recv()
    total = term[core, lo] + rs_buf[0].astype(F32) + rs_buf[1].astype(F32) + rs_buf[2].astype(F32)
    unit[...] = total.astype(BF16)

    landing = s.at[core, slab, y, pl.ds((2 * h + lo) * half_rows, half_rows)]
    far_unit = remote(unit, landing, sc_tx.at[0], sc_rx.at[core], at_device(owner, number, y, 1 - h))
    near_unit = remote(unit, landing, sc_tx.at[1], sc_rx.at[core], at_device(owner, number, y, h))
    near_local = pltpu.make_async_copy(unit, landing, sc_rx.at[core])
    send(far_unit)

    @pl.when(stays)
    def _():
        near_local.start()

    @pl.when(jnp.logical_not(stays))
    def _():
        near_unit.start()

    def near_sent():
        @pl.when(jnp.logical_not(stays))
        def _():
            near_unit.wait_send()

    later.append(near_sent)

    s_buf[core, lo] = total

    def units(ring, place, spot, pair):
        if ring == 0:
            piece = pl.ds(pl.multiple_of(place % 4 * half_rows, half_rows), half_rows)
            return s.at[0, place // 4, pl.ds(2 * spot, 2) if pair else spot, piece]
        if pair:
            return s.at[1, spot // 2, place, pl.ds(pl.multiple_of(spot % 2 * width, width), width)]
        return s.at[1, spot // 4, place, pl.ds(pl.multiple_of(spot % 4 * half_rows, half_rows), half_rows)]

    for ring in range(2):
        slot = units(ring, heres[ring], heres[1 - ring], False)
        pltpu.make_async_copy(slot, slot, sc_rx.at[ring]).wait()
        count = counts[1 - ring]
        for j in sorted(range(1, count), key=lambda j: min(j, count - j)):
            device = along(1 - ring, (heres[1 - ring] + j) % count)
            send(remote(slot, slot, first_tx.at[ring, j], first_rx.at[ring, j], device))

    for k in range(3):
        send(remote(s_buf.at[core, lo], s_buf.at[core, lo], sg_tx.at[k], sg_rx.at[k], peer(k)))
    mine = v.at[:, slab, y, pl.ds(pl.multiple_of(2 * h * half_rows, half_rows), width)]
    col_copies = [remote(mine, cols, vc_tx.at[k], vc_rx, peer(k)) for k in range(3)]
    col_local = pltpu.make_async_copy(mine, cols, vc_rx)

    @pl.when(owner == p)
    def _():
        for copy in col_copies:
            copy.start()
        col_local.start()

    def cols_sent():
        @pl.when(owner == p)
        def _():
            for copy in col_copies:
                copy.wait_send()

    later.append(cols_sent)
    hacc[...] = jnp.zeros_like(hacc)
    cross_near.wait()
    cross_buf[...] = cross_buf[...] + cross[...]
    cross_twin = remote(cross_buf, cross_far, c_tx.at[1], c_rx.at[1], peer(1))
    cross_twin.start()

    def pairs(ring):
        count = counts[1 - ring] // 2
        return [0] + [k for d in range(1, count) for k in (d, -d) if d < count - d or (d == count - d and k > 0)]

    def sent(ring, way, step, j):
        half_way, many = counts[ring] // 2, counts[1 - ring] // 2
        return step < half_way or (step == half_way and j * 2 // many == way)

    def pair_at(ring, j):
        many = counts[1 - ring] // 2
        return (heres[1 - ring] // 2 + pairs(ring)[j] + many) % many

    def ring_copy(ring, way, step, j, receiving=False):
        count, here, sign = counts[ring], heres[ring], 1 - 2 * way
        place = (here - sign * (step if receiving else step - 1) + count) % count
        index = (step - 1) * (counts[1 - ring] // 2) + j
        where = units(ring, place, pair_at(ring, j), True)
        sems = ring_tx.at[ring, way, index], ring_rx.at[ring, way, index]
        return remote(where, where, *sems, along(ring, (here + sign + count) % count))

    for j in range(max(nz, ny) // 2):
        for ring in range(2):
            count, here = counts[1 - ring], heres[1 - ring]
            if j >= count // 2:
                continue
            for spot in [2 * pair_at(ring, j), 2 * pair_at(ring, j) + 1] if j else [here // 2 * 2 + 1 - here % 2]:
                where = units(ring, heres[ring], spot, False)
                k = (here - spot + count) % count
                remote(where, where, first_tx.at[ring, k], first_rx.at[ring, k], peer(0)).wait_recv()
            for way in range(2):
                send(ring_copy(ring, way, 1, j))

    def in_two(values):
        high = values.astype(BF16)
        return jnp.concatenate([high, (values - high.astype(F32)).astype(BF16)], axis=0)

    def joined(stacked):
        return stacked[:width] + stacked[width:]

    def right_factors():
        for copy in factors:
            copy.wait()
        pltpu.make_async_copy(mine, cols, vc_rx).wait()
        second = dot(cols[1].astype(F32), f[1], 1, 1, HIGH)
        at[1] = in_two(second)
        cross_twin.wait()
        cross[...] = cross_buf[...] + cross_far[...]
        first = dot(cols[0].astype(F32) - dot(second, cross[...], 1, 1, HIGH), f[0], 1, 1, HIGH)
        at[0] = in_two(first)
        mix[...] = dot(dot(f[0], cross[...], 1, 0, HIGH), f[1], 1, 0, HIGH)
        for k, weights in enumerate((f[0], f[1], mix[...])):
            high = weights.astype(BF16)
            split[k, 0] = high
            split[k, 1] = (weights - high.astype(F32)).astype(BF16)

    def apply(ring, place):
        if ring == 0:
            tail = (place // 4, slice(None), pl.ds(pl.multiple_of(place % 4 * half_rows, half_rows), half_rows))
            many = ny * half_rows
        else:
            tail = (slice(None), place)
            many = depth * run
        piece = in_two(joined(dot(at[ring], s[(ring, *tail)].reshape(many, panel), 1, 1)))
        for k in range(2):
            hacc[k] = hacc[k] + dot(piece, v[(k, *tail)].reshape(many, panel))

    for step in range(1, max(nz, ny) // 2 + 1):
        for j in range(max(nz, ny) // 2):
            for ring in range(2):
                if j >= counts[1 - ring] // 2:
                    continue
                for way in range(2):
                    if not sent(ring, way, step, j):
                        continue
                    ring_copy(ring, way, step, j, receiving=True).wait_recv()
                    if sent(ring, way, step + 1, j):
                        send(ring_copy(ring, way, step + 1, j))
        if step == 1:
            right_factors()
            for ring in range(2):
                apply(ring, heres[ring])
        for ring in range(2):
            count, here = counts[ring], heres[ring]
            for place in (here - step + count, here + step)[: 2 if step < count // 2 else 1]:
                if step <= count // 2:
                    apply(ring, place % count)

    own = hacc[:, :width] + hacc[:, width:]
    h_near[...] = own.astype(BF16)
    near = remote(h_near, h_buf, h_tx.at[0], h_rx.at[0], peer(0))
    near.start()
    pairs_of_places = [(part, place) for part in range(depth) for place in range(0, ny, 2)]

    def right(part, place):
        spot = slice((part * ny + place) * run, (part * ny + place + 2) * run)
        update = dot(at[0], s[0, part, place : place + 2].reshape(2 * run, panel), 1, 1)
        update = update + dot(at[1], s[1, part, place : place + 2].reshape(2 * run, panel), 1, 1)
        base[:, spot] = a[:, spot].astype(F32) - joined(update)

    many = len(pairs_of_places) // 2
    for part, place in pairs_of_places[:many]:
        right(part, place)
    near.wait()
    chip = own + h_buf[...].astype(F32)
    h_send[...] = chip.astype(BF16)
    twin = remote(h_send, h_far, h_tx.at[1], h_rx.at[1], peer(1))
    twin.start()
    for k in range(3):
        mate = mates[k]
        where = s_buf.at[mate % 2, mate // 2]
        remote(where, where, sg_tx.at[k], sg_rx.at[k], peer(k)).wait_recv()
    for part, place in pairs_of_places[many:]:
        right(part, place)
    for wait in later:
        wait()
    here_rest = s_buf[...].reshape(2, width, panel) - chip
    left_one = dot(here_rest[0], f[0], 1, 0, HIGH)
    left_two = dot(here_rest[1], f[1], 1, 0, HIGH) - dot(here_rest[0], mix[...], 1, 0, HIGH)
    twin.wait()

    def times(k, panel_id):
        return dot(h_far[panel_id], split[k, 0]) + dot(h_far[panel_id], split[k, 1])

    left_one = left_one - times(0, 0)
    left_two = left_two - (times(1, 1) - times(2, 0))
    left = left_one.astype(BF16), left_two.astype(BF16)

    for part, place in pairs_of_places:
        spot = slice((part * ny + place) * run, (part * ny + place + 2) * run)
        update = dot(left[0], v[0, part, place : place + 2].reshape(2 * run, panel), 1, 1)
        update = update + dot(left[1], v[1, part, place : place + 2].reshape(2 * run, panel), 1, 1)
        out[:, spot] = (base[:, spot] - update).astype(BF16)


def body(parts, matrix, vectors_one, factor_one, vectors_two, factor_two):
    nz, ny, nh = parts
    depth = nz // ROWS
    rows, width = matrix.shape
    panel = factor_one.shape[0]
    half = width // 2
    grid = (depth, ny, 4 * half)
    hbm = pl.BlockSpec(memory_space=pltpu.HBM)
    dma = pltpu.SemaphoreType.DMA
    most = max(nz, ny)
    flops = 2 * rows * width * panel * 10
    result = pl.pallas_call(
        functools.partial(kernel, parts),
        out_shape=pltpu.VMEM((width, rows), BF16),
        in_specs=[hbm] * 5,
        out_specs=pl.BlockSpec(memory_space=pltpu.VMEM),
        scratch_shapes=[
            pltpu.VMEM((width, rows), BF16),
            pltpu.VMEM((2, *grid, panel), BF16),
            pltpu.VMEM((2, panel, panel), F32),
            pltpu.VMEM((panel, panel), F32),
            pltpu.VMEM((3, 2, panel, panel), BF16),
            pltpu.VMEM((2, width, panel), BF16),
            pltpu.VMEM((2, 2, half, panel), F32),
            pltpu.VMEM((2, 2, half, panel), BF16),
            pltpu.VMEM((3, half, panel), BF16),
            pltpu.VMEM((2, 2, half, panel), F32),
            pltpu.VMEM((half, panel), BF16),
            pltpu.VMEM((2, *grid, panel), BF16),
            pltpu.VMEM((2, width, panel), BF16),
            pltpu.VMEM((panel, panel), F32),
            pltpu.VMEM((panel, panel), F32),
            pltpu.VMEM((panel, panel), F32),
            pltpu.VMEM((2, 2 * width, panel), BF16),
            pltpu.VMEM((width, rows), F32),
            pltpu.VMEM((2, 2 * width, panel), F32),
            pltpu.VMEM((2, width, panel), BF16),
            pltpu.VMEM((2, width, panel), BF16),
            pltpu.VMEM((2, width, panel), BF16),
            dma((1 + 2 * depth,)),
            dma((2,)),
            dma((3,)),
            dma((3,)),
            dma((3,)),
            dma,
            dma((3,)),
            dma((3,)),
            dma((2,)),
            dma((2,)),
            dma((2,)),
            dma((2,)),
            dma((2,)),
            dma((2,)),
            dma((2, most)),
            dma((2, most)),
            dma((2, 2, most * most // 4)),
            dma((2, 2, most * most // 4)),
        ],
        compiler_params=pltpu.CompilerParams(
            collective_id=0, has_side_effects=True, vmem_limit_bytes=56 * 1024 * 1024
        ),
        cost_estimate=pl.CostEstimate(flops=flops, bytes_accessed=4 * rows * panel, transcendentals=0),
    )(matrix.T, vectors_one.reshape(*grid, panel), vectors_two.reshape(*grid, panel), factor_one, factor_two)
    return result.T


def build(mesh, parts):
    placed = (P("prow", "pcol"), P("prow", None), P(), P("prow", None), P())
    return jax.shard_map(
        functools.partial(body, parts), mesh=mesh, in_specs=placed, out_specs=P("prow", "pcol"), check_vma=False
    )


def solution(mesh):
    return build(mesh, PARTS)
```

```python
import functools

import jax
import jax.numpy as jnp
from jax import lax
from jax.experimental import pallas as pl
from jax.experimental.pallas import tpu as pltpu
from jax.sharding import PartitionSpec as P

MESH = pl.DeviceIdType.MESH
HIGH = lax.Precision.HIGHEST
PARTS = (8, 8, 2)
ROWS = 4
F32 = jnp.float32
BF16 = jnp.bfloat16


def dot(lhs, rhs, left=1, right=0, precision=None):
    return lax.dot_general(
        lhs, rhs, (((left,), (right,)), ((), ())), precision=precision, preferred_element_type=F32
    )


def kernel(
    parts,
    a_hbm, v1_hbm, v2_hbm, f1_hbm, f2_hbm,
    out,
    a, v, f, mix, split, h_near, term, term_send, rs_buf, s_buf, unit, s, cols, cross, cross_buf, cross_far, at, base, hacc, h_buf, h_send, h_far,
    load, f_load, rs_tx, rs_rx, vc_tx, vc_rx, sg_tx, sg_rx, sc_tx, sc_rx, c_tx, c_rx, h_tx, h_rx,
    first_tx, first_rx, ring_tx, ring_rx,
):
    nz, ny, nh = parts
    depth = nz // ROWS
    half_rows, panel = unit.shape
    width = 2 * half_rows
    run = 4 * half_rows
    p = lax.axis_index("prow")
    q = lax.axis_index("pcol")
    rem, quo = lax.rem, lax.div
    z, y, h = quo(q, ny * nh), rem(quo(q, nh), ny), rem(q, nh)
    lo, core = quo(p, 2), rem(p, 2)
    mates = (2 * lo + 1 - core, 2 * (1 - lo) + core, 3 - p)

    def at_device(row, zi, yi, hi):
        return {"prow": row, "pcol": (zi * ny + yi) * nh + hi}

    def peer(k):
        return {"prow": mates[k], "pcol": q}

    def remote(src, dst, tx, rx, device):
        return pltpu.make_async_remote_copy(
            src_ref=src, dst_ref=dst, send_sem=tx, recv_sem=rx, device_id=device, device_id_type=MESH
        )

    later = []

    def send(copy):
        copy.start()
        later.append(copy.wait_send)

    owner, slab = quo(z, depth), rem(z, depth)
    counts, heres = (nz, ny), (z, y)

    def along(ring, place):
        return at_device(p, place, y, h) if ring == 0 else at_device(p, z, place, h)

    def z_of(number, row):
        part, piece = quo(number, 4), rem(number, 4)
        reach = 2 * rem(rem(piece, 2) + quo(row, 2), 2) + quo(piece, 2)
        return rem(row * depth + part + (2 * part - 1) * reach + 2 * nz, nz)

    def unit_of(place):
        d = rem(place - p * depth + nz, nz)
        part = 1 - quo(rem(d + nz - 1, nz), 4) if depth > 1 else 0
        reach = part * (d - 1) + (1 - part) * rem(nz - d, nz)
        return part * 4 + 2 * rem(reach, 2) + rem(quo(reach, 2) + lo, 2)

    number = slab * 4 + 2 * h + lo
    to_z = z_of(number, owner)
    stays = (owner == p) & (to_z == z)
    own = unit_of(z)
    from_z, from_h, from_lo = p * depth + quo(own, 4), quo(rem(own, 4), 2), rem(own, 2)
    spots = y, own

    known = {}

    def once(key, make):
        if key not in known:
            known[key] = make()
        return known[key]

    def place_at(ring, offset):
        count = counts[ring]
        return once((ring, offset % count), lambda: rem(heres[ring] + offset % count, count))

    def home(offset):
        def make():
            unit_number = unit_of(place_at(0, offset))
            return quo(unit_number, 4), pl.multiple_of(rem(unit_number, 4) * half_rows, half_rows)

        return once(("home", offset % nz), make)

    def pair_at(ring, j):
        many = counts[1 - ring] // 2
        shift = ([0, 1] if many < 4 else [0, 1, 3, 2])[j]
        return once(("pair", ring, j), lambda: rem(quo(spots[ring], 2) + shift, many))

    def pair_rows(j):
        make = lambda: (quo(pair_at(1, j), 2), pl.multiple_of(rem(pair_at(1, j), 2) * width, width))
        return once(("rows", j), make)

    def place_of(ring, spot):
        return spot if ring == 0 else z_of(spot, p)

    stretch = ny * run
    cuts = [(part, cut) for part in range(depth) for cut in range(2)]
    a_loads = []
    v_loads = []
    for place, (part, cut) in enumerate(cuts):
        lanes = slice((2 * part + cut) * stretch // 2, (2 * part + cut + 1) * stretch // 2)
        middle = slice(cut * ny // 2, (cut + 1) * ny // 2)
        a_loads.append(pltpu.make_async_copy(a_hbm.at[:, lanes], a.at[:, lanes], load.at[0, place]))
        v_loads.append(
            [
                pltpu.make_async_copy(source.at[part, middle], v.at[k, part, middle], load.at[1 + k, place])
                for k, source in enumerate((v1_hbm, v2_hbm))
            ]
        )
        for copy in (a_loads[-1], *v_loads[-1]):
            copy.start()
    factors = [pltpu.make_async_copy((f1_hbm, f2_hbm)[k], f.at[k], f_load.at[k]) for k in range(2)]
    for copy in factors:
        copy.start()

    barrier = pltpu.get_barrier_semaphore()

    def greet(device):
        pl.semaphore_signal(barrier, inc=1, device_id=device, device_id_type=MESH)

    for k in range(3):
        greet(peer(k))
    for ring in range(2):
        for k in range(1, counts[ring]):
            greet(along(ring, place_at(ring, k)))
    for k in range(2):
        from_p = 2 * from_lo + k

        @pl.when(jnp.logical_not((from_p == p) & (from_z == z) & (from_h == h)))
        def _():
            greet(at_device(from_p, from_z, y, from_h))

    sums = [None, None]
    for place, (part, cut) in enumerate(cuts):
        lanes = slice((2 * part + cut) * stretch // 2, (2 * part + cut + 1) * stretch // 2)
        a_loads[place].wait()
        for k in range(2):
            v_loads[place][k].wait()
            vectors = v[k, part, cut * ny // 2 : (cut + 1) * ny // 2].reshape(stretch // 2, panel)
            more = dot(a[:, lanes], vectors)
            sums[k] = more if sums[k] is None else sums[k] + more
    for k in range(2):
        term[k] = sums[k].reshape(2, half_rows, panel)
        term_send[k] = sums[k].reshape(2, half_rows, panel).astype(BF16)

    pl.semaphore_wait(barrier, 3 + (ny - 1) + (nz - 1) + 2 - jnp.where(stays, 1, 0))

    scattered = []
    for k in (2, 1, 0):
        mate = mates[k]
        copy = remote(term_send.at[mate % 2, mate // 2], rs_buf.at[k], rs_tx.at[k], rs_rx.at[k], peer(k))
        send(copy)
        scattered.append(copy)

    for copy in scattered:
        copy.wait_recv()
    total = term[core, lo] + rs_buf[0].astype(F32) + rs_buf[1].astype(F32) + rs_buf[2].astype(F32)
    unit[...] = total.astype(BF16)

    landing = s.at[core, slab, y, pl.ds((2 * h + lo) * half_rows, half_rows)]
    far_unit = remote(unit, landing, sc_tx.at[0], sc_rx.at[core], at_device(owner, to_z, y, 1 - h))
    near_unit = remote(unit, landing, sc_tx.at[1], sc_rx.at[core], at_device(owner, to_z, y, h))
    near_local = pltpu.make_async_copy(unit, landing, sc_rx.at[core])
    send(far_unit)

    @pl.when(stays)
    def _():
        near_local.start()

    @pl.when(jnp.logical_not(stays))
    def _():
        near_unit.start()

    def near_sent():
        @pl.when(jnp.logical_not(stays))
        def _():
            near_unit.wait_send()

    later.append(near_sent)

    s_buf[core, lo] = total

    rows = depth * stretch
    cross[...] = dot(v[0].reshape(rows, panel), v[1].reshape(rows, panel), 0, 0)
    cross_near = remote(cross, cross_buf, c_tx.at[0], c_rx.at[0], peer(0))
    cross_near.start()

    def units(ring, offset, spot):
        if ring == 0:
            part, first = home(offset)
            return s.at[0, part, spot, pl.ds(first, half_rows)]
        first = pl.multiple_of(rem(spot, 4) * half_rows, half_rows)
        return s.at[1, quo(spot, 4), place_at(1, offset), pl.ds(first, half_rows)]

    def two_units(ring, offset, j):
        if ring == 0:
            part, first = home(offset)
            return s.at[0, part, pl.ds(2 * pair_at(0, j), 2), pl.ds(first, half_rows)]
        part, first = pair_rows(j)
        return s.at[1, part, place_at(1, offset), pl.ds(first, width)]

    for ring in range(2):
        slot = units(ring, 0, spots[ring])
        pltpu.make_async_copy(slot, slot, sc_rx.at[ring]).wait()
        count = counts[1 - ring]
        for j in sorted(range(1, count), key=lambda j: min(j, count - j)):
            device = along(1 - ring, place_at(1 - ring, j))
            send(remote(slot, slot, first_tx.at[ring, j], first_rx.at[ring, j], device))

    for k in range(3):
        send(remote(s_buf.at[core, lo], s_buf.at[core, lo], sg_tx.at[k], sg_rx.at[k], peer(k)))
    mine = v.at[:, slab, y, pl.ds(pl.multiple_of(2 * h * half_rows, half_rows), width)]
    col_copies = [remote(mine, cols, vc_tx.at[k], vc_rx, peer(k)) for k in range(3)]
    col_local = pltpu.make_async_copy(mine, cols, vc_rx)

    @pl.when(owner == p)
    def _():
        for copy in col_copies:
            copy.start()
        col_local.start()

    def cols_sent():
        @pl.when(owner == p)
        def _():
            for copy in col_copies:
                copy.wait_send()

    later.append(cols_sent)
    hacc[...] = jnp.zeros_like(hacc)
    cross_near.wait()
    cross_buf[...] = cross_buf[...] + cross[...]
    cross_twin = remote(cross_buf, cross_far, c_tx.at[1], c_rx.at[1], peer(1))
    cross_twin.start()

    def sent(ring, way, step, j):
        half_way, many = counts[ring] // 2, counts[1 - ring] // 2
        return step < half_way or (step == half_way and j * 2 // many == way)

    def ring_copy(ring, way, step, j, receiving=False):
        sign = 1 - 2 * way
        index = (step - 1) * (counts[1 - ring] // 2) + j
        where = two_units(ring, -sign * (step if receiving else step - 1), j)
        sems = ring_tx.at[ring, way, index], ring_rx.at[ring, way, index]
        return remote(where, where, *sems, along(ring, place_at(ring, sign)))

    for j in range(max(nz, ny) // 2):
        for ring in range(2):
            count, here = counts[1 - ring], heres[1 - ring]
            if j >= count // 2:
                continue
            mine_too = once(("odd", ring), lambda: rem(spots[ring], 2))
            for spot in [2 * pair_at(ring, j) + 1 - mine_too] + ([2 * pair_at(ring, j) + mine_too] if j else []):
                where = units(ring, 0, spot)
                k = rem(here - place_of(ring, spot) + count, count)
                remote(where, where, first_tx.at[ring, k], first_rx.at[ring, k], peer(0)).wait_recv()
            for way in range(2):
                send(ring_copy(ring, way, 1, j))

    def in_two(values):
        high = values.astype(BF16)
        return jnp.concatenate([high, (values - high.astype(F32)).astype(BF16)], axis=0)

    def joined(stacked):
        return stacked[:width] + stacked[width:]

    def right_factors():
        for copy in factors:
            copy.wait()
        pltpu.make_async_copy(mine, cols, vc_rx).wait()
        second = dot(cols[1].astype(F32), f[1], 1, 1, HIGH)
        at[1] = in_two(second)
        cross_twin.wait()
        cross[...] = cross_buf[...] + cross_far[...]
        first = dot(cols[0].astype(F32) - dot(second, cross[...], 1, 1, HIGH), f[0], 1, 1, HIGH)
        at[0] = in_two(first)
        mix[...] = dot(dot(f[0], cross[...], 1, 0, HIGH), f[1], 1, 0, HIGH)
        for k, weights in enumerate((f[0], f[1], mix[...])):
            high = weights.astype(BF16)
            split[k, 0] = high
            split[k, 1] = (weights - high.astype(F32)).astype(BF16)

    def apply(ring, offset):
        if ring == 0:
            part, first = home(offset)
            tail = (part, slice(None), pl.ds(first, half_rows))
            many = ny * half_rows
        else:
            tail = (slice(None), place_at(1, offset))
            many = depth * run
        piece = in_two(joined(dot(at[ring], s[(ring, *tail)].reshape(many, panel), 1, 1)))
        for k in range(2):
            hacc[k] = hacc[k] + dot(piece, v[(k, *tail)].reshape(many, panel))

    ready = [right_factors, *(functools.partial(apply, ring, 0) for ring in range(2))]
    turns = max(nz, ny) // 2
    for step in range(1, turns + 1):
        for j in range(turns):
            for ring in range(2):
                if j >= counts[1 - ring] // 2:
                    continue
                for way in range(2):
                    if not sent(ring, way, step, j):
                        continue
                    ring_copy(ring, way, step, j, receiving=True).wait_recv()
                    if sent(ring, way, step + 1, j):
                        send(ring_copy(ring, way, step + 1, j))
            if step == 1 and j == 0:
                continue
            for _ in range(-(-len(ready) // (turns - j))):
                ready.pop(0)()
        for ring in range(2):
            half_way = counts[ring] // 2
            for offset in (-step, step)[: 2 if step < half_way else 1 if step == half_way else 0]:
                ready.append(functools.partial(apply, ring, offset))
    for work in ready:
        work()

    summed = hacc[:, :width] + hacc[:, width:]
    h_near[...] = summed.astype(BF16)
    near = remote(h_near, h_buf, h_tx.at[0], h_rx.at[0], peer(0))
    near.start()
    pairs_of_places = [(part, place) for part in range(depth) for place in range(0, ny, 2)]

    def right(part, place):
        spot = slice((part * ny + place) * run, (part * ny + place + 2) * run)
        update = dot(at[0], s[0, part, place : place + 2].reshape(2 * run, panel), 1, 1)
        update = update + dot(at[1], s[1, part, place : place + 2].reshape(2 * run, panel), 1, 1)
        base[:, spot] = a[:, spot].astype(F32) - joined(update)

    many = len(pairs_of_places) // 2
    for part, place in pairs_of_places[:many]:
        right(part, place)
    near.wait()
    chip = summed + h_buf[...].astype(F32)
    h_send[...] = chip.astype(BF16)
    twin = remote(h_send, h_far, h_tx.at[1], h_rx.at[1], peer(1))
    twin.start()
    for k in range(3):
        mate = mates[k]
        where = s_buf.at[mate % 2, mate // 2]
        remote(where, where, sg_tx.at[k], sg_rx.at[k], peer(k)).wait_recv()
    for part, place in pairs_of_places[many:]:
        right(part, place)
    for wait in later:
        wait()
    here_rest = s_buf[...].reshape(2, width, panel) - chip
    left_one = dot(here_rest[0], f[0], 1, 0, HIGH)
    left_two = dot(here_rest[1], f[1], 1, 0, HIGH) - dot(here_rest[0], mix[...], 1, 0, HIGH)
    twin.wait()

    def times(k, panel_id):
        return dot(h_far[panel_id], split[k, 0]) + dot(h_far[panel_id], split[k, 1])

    left_one = left_one - times(0, 0)
    left_two = left_two - (times(1, 1) - times(2, 0))
    left = in_two(left_one), in_two(left_two)

    for part, place in pairs_of_places:
        spot = slice((part * ny + place) * run, (part * ny + place + 2) * run)
        update = dot(left[0], v[0, part, place : place + 2].reshape(2 * run, panel), 1, 1)
        update = update + dot(left[1], v[1, part, place : place + 2].reshape(2 * run, panel), 1, 1)
        out[:, spot] = (base[:, spot] - joined(update)).astype(BF16)


def body(parts, matrix, vectors_one, factor_one, vectors_two, factor_two):
    nz, ny, nh = parts
    depth = nz // ROWS
    rows, width = matrix.shape
    panel = factor_one.shape[0]
    half = width // 2
    grid = (depth, ny, 4 * half)
    hbm = pl.BlockSpec(memory_space=pltpu.HBM)
    dma = pltpu.SemaphoreType.DMA
    most = max(nz, ny)
    flops = 2 * rows * width * panel * 10
    result = pl.pallas_call(
        functools.partial(kernel, parts),
        out_shape=pltpu.VMEM((width, rows), BF16),
        in_specs=[hbm] * 5,
        out_specs=pl.BlockSpec(memory_space=pltpu.VMEM),
        scratch_shapes=[
            pltpu.VMEM((width, rows), BF16),
            pltpu.VMEM((2, *grid, panel), BF16),
            pltpu.VMEM((2, panel, panel), F32),
            pltpu.VMEM((panel, panel), F32),
            pltpu.VMEM((3, 2, panel, panel), BF16),
            pltpu.VMEM((2, width, panel), BF16),
            pltpu.VMEM((2, 2, half, panel), F32),
            pltpu.VMEM((2, 2, half, panel), BF16),
            pltpu.VMEM((3, half, panel), BF16),
            pltpu.VMEM((2, 2, half, panel), F32),
            pltpu.VMEM((half, panel), BF16),
            pltpu.VMEM((2, *grid, panel), BF16),
            pltpu.VMEM((2, width, panel), BF16),
            pltpu.VMEM((panel, panel), F32),
            pltpu.VMEM((panel, panel), F32),
            pltpu.VMEM((panel, panel), F32),
            pltpu.VMEM((2, 2 * width, panel), BF16),
            pltpu.VMEM((width, rows), F32),
            pltpu.VMEM((2, 2 * width, panel), F32),
            pltpu.VMEM((2, width, panel), BF16),
            pltpu.VMEM((2, width, panel), BF16),
            pltpu.VMEM((2, width, panel), BF16),
            dma((3, 2 * depth)),
            dma((2,)),
            dma((3,)),
            dma((3,)),
            dma((3,)),
            dma,
            dma((3,)),
            dma((3,)),
            dma((2,)),
            dma((2,)),
            dma((2,)),
            dma((2,)),
            dma((2,)),
            dma((2,)),
            dma((2, most)),
            dma((2, most)),
            dma((2, 2, most * most // 4)),
            dma((2, 2, most * most // 4)),
        ],
        compiler_params=pltpu.CompilerParams(
            collective_id=0, has_side_effects=True, vmem_limit_bytes=56 * 1024 * 1024
        ),
        cost_estimate=pl.CostEstimate(flops=flops, bytes_accessed=4 * rows * panel, transcendentals=0),
    )(matrix.T, vectors_one.reshape(*grid, panel), vectors_two.reshape(*grid, panel), factor_one, factor_two)
    return result.T


def build(mesh, parts):
    placed = (P("prow", "pcol"), P("prow", None), P(), P("prow", None), P())
    return jax.shard_map(
        functools.partial(body, parts), mesh=mesh, in_specs=placed, out_specs=P("prow", "pcol"), check_vma=False
    )


def solution(mesh):
    return build(mesh, PARTS)
```

```python
import functools

import jax
import jax.numpy as jnp
from jax import lax
from jax.experimental import pallas as pl
from jax.experimental.pallas import tpu as pltpu
from jax.sharding import PartitionSpec as P

MESH = pl.DeviceIdType.MESH
HIGH = lax.Precision.HIGHEST
PARTS = (8, 8, 2)
ROWS = 4
F32 = jnp.float32
BF16 = jnp.bfloat16


def dot(lhs, rhs, left=1, right=0, precision=None):
    return lax.dot_general(
        lhs, rhs, (((left,), (right,)), ((), ())), precision=precision, preferred_element_type=F32
    )


def kernel(
    parts,
    a_hbm, v1_hbm, v2_hbm, f1_hbm, f2_hbm,
    out,
    a, v, f, mix, split, h_near, term, term_send, rs_buf, s_buf, unit, s, cols, cross, cross_buf, cross_far, at, base, hacc, h_buf, h_send, h_far,
    load, f_load, rs_tx, rs_rx, vc_tx, vc_rx, sg_tx, sg_rx, sc_tx, sc_rx, c_tx, c_rx, h_tx, h_rx,
    first_tx, first_rx, ring_tx, ring_rx,
):
    nz, ny, nh = parts
    depth = nz // ROWS
    half_rows, panel = unit.shape
    width = 2 * half_rows
    run = 4 * half_rows
    p = lax.axis_index("prow")
    q = lax.axis_index("pcol")
    rem, quo = lax.rem, lax.div
    z, y, h = quo(q, ny * nh), rem(quo(q, nh), ny), rem(q, nh)
    lo, core = quo(p, 2), rem(p, 2)
    mates = (2 * lo + 1 - core, 2 * (1 - lo) + core, 3 - p)

    def at_device(row, zi, yi, hi):
        return {"prow": row, "pcol": (zi * ny + yi) * nh + hi}

    def peer(k):
        return {"prow": mates[k], "pcol": q}

    def remote(src, dst, tx, rx, device):
        return pltpu.make_async_remote_copy(
            src_ref=src, dst_ref=dst, send_sem=tx, recv_sem=rx, device_id=device, device_id_type=MESH
        )

    later = []

    def send(copy):
        copy.start()
        later.append(copy.wait_send)

    owner, slab = quo(z, depth), rem(z, depth)
    counts, heres = (nz, ny), (z, y)

    def along(ring, place):
        return at_device(p, place, y, h) if ring == 0 else at_device(p, z, place, h)

    def z_of(number, row):
        part, piece = quo(number, 4), rem(number, 4)
        reach = 2 * rem(rem(piece, 2) + quo(row, 2), 2) + quo(piece, 2)
        return rem(row * depth + part + (2 * part - 1) * reach + 2 * nz, nz)

    def unit_of(place):
        d = rem(place - p * depth + nz, nz)
        part = 1 - quo(rem(d + nz - 1, nz), 4) if depth > 1 else 0
        reach = part * (d - 1) + (1 - part) * rem(nz - d, nz)
        return part * 4 + 2 * rem(reach, 2) + rem(quo(reach, 2) + lo, 2)

    number = slab * 4 + 2 * h + lo
    to_z = z_of(number, owner)
    stays = (owner == p) & (to_z == z)
    own = unit_of(z)
    from_z, from_h, from_lo = p * depth + quo(own, 4), quo(rem(own, 4), 2), rem(own, 2)
    spots = y, own

    known = {}

    def once(key, make):
        if key not in known:
            known[key] = make()
        return known[key]

    def place_at(ring, offset):
        count = counts[ring]
        return once((ring, offset % count), lambda: rem(heres[ring] + offset % count, count))

    def home(offset):
        def make():
            unit_number = unit_of(place_at(0, offset))
            return quo(unit_number, 4), pl.multiple_of(rem(unit_number, 4) * half_rows, half_rows)

        return once(("home", offset % nz), make)

    def pair_at(ring, j):
        many = counts[1 - ring] // 2
        shift = ([0, 1] if many < 4 else [0, 1, 3, 2])[j]
        return once(("pair", ring, j), lambda: rem(quo(spots[ring], 2) + shift, many))

    def pair_rows(j):
        make = lambda: (quo(pair_at(1, j), 2), pl.multiple_of(rem(pair_at(1, j), 2) * width, width))
        return once(("rows", j), make)

    def place_of(ring, spot):
        return spot if ring == 0 else z_of(spot, p)

    stretch = ny * run
    cuts = [(part, cut) for part in range(depth) for cut in range(2)]
    a_loads = []
    v_loads = []
    for place, (part, cut) in enumerate(cuts):
        lanes = slice((2 * part + cut) * stretch // 2, (2 * part + cut + 1) * stretch // 2)
        middle = slice(cut * ny // 2, (cut + 1) * ny // 2)
        a_loads.append(pltpu.make_async_copy(a_hbm.at[:, lanes], a.at[:, lanes], load.at[0, place]))
        v_loads.append(
            [
                pltpu.make_async_copy(source.at[part, middle], v.at[k, part, middle], load.at[1 + k, place])
                for k, source in enumerate((v1_hbm, v2_hbm))
            ]
        )
        for copy in (a_loads[-1], *v_loads[-1]):
            copy.start()
    factors = [pltpu.make_async_copy((f1_hbm, f2_hbm)[k], f.at[k], f_load.at[k]) for k in range(2)]
    for copy in factors:
        copy.start()

    barrier = pltpu.get_barrier_semaphore()

    def greet(device):
        pl.semaphore_signal(barrier, inc=1, device_id=device, device_id_type=MESH)

    for k in range(3):
        greet(peer(k))
    for ring in range(2):
        for k in range(1, counts[ring]):
            greet(along(ring, place_at(ring, k)))
    for k in range(2):
        from_p = 2 * from_lo + k

        @pl.when(jnp.logical_not((from_p == p) & (from_z == z) & (from_h == h)))
        def _():
            greet(at_device(from_p, from_z, y, from_h))

    sums = [None, None]
    for place, (part, cut) in enumerate(cuts):
        lanes = slice((2 * part + cut) * stretch // 2, (2 * part + cut + 1) * stretch // 2)
        a_loads[place].wait()
        for k in range(2):
            v_loads[place][k].wait()
            vectors = v[k, part, cut * ny // 2 : (cut + 1) * ny // 2].reshape(stretch // 2, panel)
            more = dot(a[:, lanes], vectors)
            sums[k] = more if sums[k] is None else sums[k] + more
    for k in range(2):
        term[k] = sums[k].reshape(2, half_rows, panel)
        term_send[k] = sums[k].reshape(2, half_rows, panel).astype(BF16)

    pl.semaphore_wait(barrier, 3 + (ny - 1) + (nz - 1) + 2 - jnp.where(stays, 1, 0))

    scattered = []
    for k in (2, 1, 0):
        mate = mates[k]
        copy = remote(term_send.at[mate % 2, mate // 2], rs_buf.at[k], rs_tx.at[k], rs_rx.at[k], peer(k))
        send(copy)
        scattered.append(copy)

    for copy in scattered:
        copy.wait_recv()
    total = term[core, lo] + rs_buf[0].astype(F32) + rs_buf[1].astype(F32) + rs_buf[2].astype(F32)
    unit[...] = total.astype(BF16)

    landing = s.at[core, slab, y, pl.ds((2 * h + lo) * half_rows, half_rows)]
    far_unit = remote(unit, landing, sc_tx.at[0], sc_rx.at[core], at_device(owner, to_z, y, 1 - h))
    near_unit = remote(unit, landing, sc_tx.at[1], sc_rx.at[core], at_device(owner, to_z, y, h))
    near_local = pltpu.make_async_copy(unit, landing, sc_rx.at[core])
    send(far_unit)

    @pl.when(stays)
    def _():
        near_local.start()

    @pl.when(jnp.logical_not(stays))
    def _():
        near_unit.start()

    def near_sent():
        @pl.when(jnp.logical_not(stays))
        def _():
            near_unit.wait_send()

    later.append(near_sent)

    s_buf[core, lo] = total

    rows = depth * stretch
    cross[...] = dot(v[0].reshape(rows, panel), v[1].reshape(rows, panel), 0, 0)
    cross_near = remote(cross, cross_buf, c_tx.at[0], c_rx.at[0], peer(0))
    cross_near.start()

    def units(ring, offset, spot):
        if ring == 0:
            part, first = home(offset)
            return s.at[0, part, spot, pl.ds(first, half_rows)]
        first = pl.multiple_of(rem(spot, 4) * half_rows, half_rows)
        return s.at[1, quo(spot, 4), place_at(1, offset), pl.ds(first, half_rows)]

    def two_units(ring, offset, j):
        if ring == 0:
            part, first = home(offset)
            return s.at[0, part, pl.ds(2 * pair_at(0, j), 2), pl.ds(first, half_rows)]
        part, first = pair_rows(j)
        return s.at[1, part, place_at(1, offset), pl.ds(first, width)]

    for ring in range(2):
        slot = units(ring, 0, spots[ring])
        pltpu.make_async_copy(slot, slot, sc_rx.at[ring]).wait()
        count = counts[1 - ring]
        for j in sorted(range(1, count), key=lambda j: min(j, count - j)):
            device = along(1 - ring, place_at(1 - ring, j))
            send(remote(slot, slot, first_tx.at[ring, j], first_rx.at[ring, j], device))

    for k in range(3):
        send(remote(s_buf.at[core, lo], s_buf.at[core, lo], sg_tx.at[k], sg_rx.at[k], peer(k)))
    mine = v.at[:, slab, y, pl.ds(pl.multiple_of(2 * h * half_rows, half_rows), width)]
    col_copies = [remote(mine, cols, vc_tx.at[k], vc_rx, peer(k)) for k in range(3)]
    col_local = pltpu.make_async_copy(mine, cols, vc_rx)

    @pl.when(owner == p)
    def _():
        for copy in col_copies:
            copy.start()
        col_local.start()

    def cols_sent():
        @pl.when(owner == p)
        def _():
            for copy in col_copies:
                copy.wait_send()

    later.append(cols_sent)
    hacc[...] = jnp.zeros_like(hacc)
    cross_near.wait()
    cross_buf[...] = cross_buf[...] + cross[...]
    cross_twin = remote(cross_buf, cross_far, c_tx.at[1], c_rx.at[1], peer(1))
    cross_twin.start()

    def sent(ring, way, step, j):
        half_way, many = counts[ring] // 2, counts[1 - ring] // 2
        return step < half_way or (step == half_way and j * 2 // many == way)

    def ring_copy(ring, way, step, j, receiving=False):
        sign = 1 - 2 * way
        index = (step - 1) * (counts[1 - ring] // 2) + j
        where = two_units(ring, -sign * (step if receiving else step - 1), j)
        sems = ring_tx.at[ring, way, index], ring_rx.at[ring, way, index]
        return remote(where, where, *sems, along(ring, place_at(ring, sign)))

    for j in range(max(nz, ny) // 2):
        for ring in range(2):
            count, here = counts[1 - ring], heres[1 - ring]
            if j >= count // 2:
                continue
            mine_too = once(("odd", ring), lambda: rem(spots[ring], 2))
            for spot in [2 * pair_at(ring, j) + 1 - mine_too] + ([2 * pair_at(ring, j) + mine_too] if j else []):
                where = units(ring, 0, spot)
                k = rem(here - place_of(ring, spot) + count, count)
                remote(where, where, first_tx.at[ring, k], first_rx.at[ring, k], peer(0)).wait_recv()
            for way in range(2):
                send(ring_copy(ring, way, 1, j))

    def in_two(values):
        high = values.astype(BF16)
        return jnp.concatenate([high, (values - high.astype(F32)).astype(BF16)], axis=0)

    def joined(stacked):
        return stacked[:width] + stacked[width:]

    def right_factors():
        for copy in factors:
            copy.wait()
        pltpu.make_async_copy(mine, cols, vc_rx).wait()
        second = dot(cols[1].astype(F32), f[1], 1, 1, HIGH)
        at[1] = in_two(second)
        cross_twin.wait()
        cross[...] = cross_buf[...] + cross_far[...]
        first = dot(cols[0].astype(F32) - dot(second, cross[...], 1, 1, HIGH), f[0], 1, 1, HIGH)
        at[0] = in_two(first)
        mix[...] = dot(dot(f[0], cross[...], 1, 0, HIGH), f[1], 1, 0, HIGH)
        for k, weights in enumerate((f[0], f[1], mix[...])):
            high = weights.astype(BF16)
            split[k, 0] = high
            split[k, 1] = (weights - high.astype(F32)).astype(BF16)

    def apply(ring, offset):
        if ring == 0:
            part, first = home(offset)
            tail = (part, slice(None), pl.ds(first, half_rows))
            many = ny * half_rows
        else:
            tail = (slice(None), place_at(1, offset))
            many = depth * run
        piece = in_two(joined(dot(at[ring], s[(ring, *tail)].reshape(many, panel), 1, 1)))
        for k in range(2):
            hacc[k] = hacc[k] + dot(piece, v[(k, *tail)].reshape(many, panel))

    ready = [right_factors, *(functools.partial(apply, ring, 0) for ring in range(2))]
    turns = max(nz, ny) // 2
    for step in range(1, turns + 1):
        for j in range(turns):
            for ring in range(2):
                if j >= counts[1 - ring] // 2:
                    continue
                for way in range(2):
                    if not sent(ring, way, step, j):
                        continue
                    ring_copy(ring, way, step, j, receiving=True).wait_recv()
                    if sent(ring, way, step + 1, j):
                        send(ring_copy(ring, way, step + 1, j))
            if step == 1 and j == 0:
                continue
            for _ in range(-(-len(ready) // (turns - j))):
                ready.pop(0)()
        for ring in range(2):
            half_way = counts[ring] // 2
            for offset in (-step, step)[: 2 if step < half_way else 1 if step == half_way else 0]:
                ready.append(functools.partial(apply, ring, offset))
    for work in ready:
        work()

    summed = hacc[:, :width] + hacc[:, width:]
    h_near[...] = summed.astype(BF16)
    near = remote(h_near, h_buf, h_tx.at[0], h_rx.at[0], peer(0))
    near.start()
    pairs_of_places = [(part, place) for part in range(depth) for place in range(0, ny, 2)]

    def right(part, place):
        spot = slice((part * ny + place) * run, (part * ny + place + 2) * run)
        update = dot(at[0], s[0, part, place : place + 2].reshape(2 * run, panel), 1, 1)
        update = update + dot(at[1], s[1, part, place : place + 2].reshape(2 * run, panel), 1, 1)
        base[:, spot] = a[:, spot].astype(F32) - joined(update)

    many = len(pairs_of_places) // 2
    for part, place in pairs_of_places[:many]:
        right(part, place)
    near.wait()
    chip = summed + h_buf[...].astype(F32)
    h_send[...] = chip.astype(BF16)
    twin = remote(h_send, h_far, h_tx.at[1], h_rx.at[1], peer(1))
    twin.start()
    for k in range(3):
        mate = mates[k]
        where = s_buf.at[mate % 2, mate // 2]
        remote(where, where, sg_tx.at[k], sg_rx.at[k], peer(k)).wait_recv()
    for part, place in pairs_of_places[many:]:
        right(part, place)
    for wait in later:
        wait()
    here_rest = s_buf[...].reshape(2, width, panel) - chip
    left_one = dot(here_rest[0], f[0], 1, 0, HIGH)
    left_two = dot(here_rest[1], f[1], 1, 0, HIGH) - dot(here_rest[0], mix[...], 1, 0, HIGH)
    twin.wait()

    def times(k, panel_id):
        return dot(h_far[panel_id], split[k, 0]) + dot(h_far[panel_id], split[k, 1])

    left_one = left_one - times(0, 0)
    left_two = left_two - (times(1, 1) - times(2, 0))
    left = left_one.astype(BF16), left_two.astype(BF16)

    for part, place in pairs_of_places:
        spot = slice((part * ny + place) * run, (part * ny + place + 2) * run)
        update = dot(left[0], v[0, part, place : place + 2].reshape(2 * run, panel), 1, 1)
        update = update + dot(left[1], v[1, part, place : place + 2].reshape(2 * run, panel), 1, 1)
        out[:, spot] = (base[:, spot] - update).astype(BF16)


def body(parts, matrix, vectors_one, factor_one, vectors_two, factor_two):
    nz, ny, nh = parts
    depth = nz // ROWS
    rows, width = matrix.shape
    panel = factor_one.shape[0]
    half = width // 2
    grid = (depth, ny, 4 * half)
    hbm = pl.BlockSpec(memory_space=pltpu.HBM)
    dma = pltpu.SemaphoreType.DMA
    most = max(nz, ny)
    flops = 2 * rows * width * panel * 10
    result = pl.pallas_call(
        functools.partial(kernel, parts),
        out_shape=pltpu.VMEM((width, rows), BF16),
        in_specs=[hbm] * 5,
        out_specs=pl.BlockSpec(memory_space=pltpu.VMEM),
        scratch_shapes=[
            pltpu.VMEM((width, rows), BF16),
            pltpu.VMEM((2, *grid, panel), BF16),
            pltpu.VMEM((2, panel, panel), F32),
            pltpu.VMEM((panel, panel), F32),
            pltpu.VMEM((3, 2, panel, panel), BF16),
            pltpu.VMEM((2, width, panel), BF16),
            pltpu.VMEM((2, 2, half, panel), F32),
            pltpu.VMEM((2, 2, half, panel), BF16),
            pltpu.VMEM((3, half, panel), BF16),
            pltpu.VMEM((2, 2, half, panel), F32),
            pltpu.VMEM((half, panel), BF16),
            pltpu.VMEM((2, *grid, panel), BF16),
            pltpu.VMEM((2, width, panel), BF16),
            pltpu.VMEM((panel, panel), F32),
            pltpu.VMEM((panel, panel), F32),
            pltpu.VMEM((panel, panel), F32),
            pltpu.VMEM((2, 2 * width, panel), BF16),
            pltpu.VMEM((width, rows), F32),
            pltpu.VMEM((2, 2 * width, panel), F32),
            pltpu.VMEM((2, width, panel), BF16),
            pltpu.VMEM((2, width, panel), BF16),
            pltpu.VMEM((2, width, panel), BF16),
            dma((3, 2 * depth)),
            dma((2,)),
            dma((3,)),
            dma((3,)),
            dma((3,)),
            dma,
            dma((3,)),
            dma((3,)),
            dma((2,)),
            dma((2,)),
            dma((2,)),
            dma((2,)),
            dma((2,)),
            dma((2,)),
            dma((2, most)),
            dma((2, most)),
            dma((2, 2, most * most // 4)),
            dma((2, 2, most * most // 4)),
        ],
        compiler_params=pltpu.CompilerParams(
            collective_id=0, has_side_effects=True, vmem_limit_bytes=56 * 1024 * 1024
        ),
        cost_estimate=pl.CostEstimate(flops=flops, bytes_accessed=4 * rows * panel, transcendentals=0),
    )(matrix.T, vectors_one.reshape(*grid, panel), vectors_two.reshape(*grid, panel), factor_one, factor_two)
    return result.T


def build(mesh, parts):
    placed = (P("prow", "pcol"), P("prow", None), P(), P("prow", None), P())
    return jax.shard_map(
        functools.partial(body, parts), mesh=mesh, in_specs=placed, out_specs=P("prow", "pcol"), check_vma=False
    )


def solution(mesh):
    return build(mesh, PARTS)
```
